256 devices in a mesh: depth: 8 (over z_lo, y), row: 8 (over z_hi, core), col: 4 (over x).
Axes of the slice: x: 4, y: 4, z: 8 (z_hi: 4, z_lo: 2; z = z_hi * 2 + z_lo), core: 2. Of those that a mesh axis runs over, the one named last changes fastest.
Arguments:
- tokens: bfloat16 [768, 6144], P(('depth', 'col'), 'row'), may hold values from -6 to 6
- cotangent: bfloat16 [768, 6144], P(('depth', 'col'), 'row'), may hold values from -6 to 6
- gate_weight: bfloat16 [6144, 24576], P('row', ('depth', 'col')), may hold values from -0.078125 to 0.078125
- up_weight: bfloat16 [6144, 24576], P('row', ('depth', 'col')), may hold values from -0.078125 to 0.078125
- down_weight: bfloat16 [24576, 6144], P(('depth', 'col'), 'row'), may hold values from -0.0390625 to 0.0390625
Outputs:
- output: bfloat16 [768, 6144], P(('depth', 'col'), 'row')
- grad_tokens: bfloat16 [768, 6144], P(('depth', 'col'), 'row')
- grad_gate: bfloat16 [6144, 24576], P('row', ('depth', 'col'))
- grad_up: bfloat16 [6144, 24576], P('row', ('depth', 'col'))
- grad_down: bfloat16 [24576, 6144], P(('depth', 'col'), 'row')
The draws below stay inside these ranges and needn't reach their ends.
All inputs are finite; a program needn't handle non-finite values.
Results may differ from the reference program's by a relative error of at most 0.005.
Values may be sent and summed in bfloat16 or wider, within the bound.
A program may use at most 64 MiB of HBM per device.

```python
import jax
import jax.numpy as jnp

D = 6144
FF = 24576
TOKENS = 768


def levels(key, dims, split, least, largest):
    gain = 1.0
    for axis_at, parts in split:
        draws = jax.random.uniform(jax.random.fold_in(jax.random.fold_in(key, 6), axis_at), (parts,), jnp.float32, least / len(split), largest / len(split))
        gain = gain * jnp.repeat(jnp.exp(draws), dims[axis_at] // parts).reshape((-1,) + (1,) * (len(dims) - 1 - axis_at))
    return gain


def centred(rng, shape, scale, reach, split=(), dtype=jnp.bfloat16):
    result = jax.random.normal(rng, shape, jnp.float32) * scale
    if len(split) > 0:
        result = levels(rng, shape, split, -0.22, 0.18) * result
    return jnp.clip(result, min=-reach, max=reach).astype(dtype)


def setup_inputs(seed: int = 0) -> dict:
    splits = jax.random.split(jax.random.key(seed), 6)
    tokens = centred(splits[0], (TOKENS, D), 1.0, 6.0, ((0, 32), (1, 8)))
    cotangent = centred(splits[1], (TOKENS, D), 1.0, 6.0, ((0, 32), (1, 8)))
    gate_weight = centred(splits[2], (D, FF), D ** -0.5, 0.078125, ((0, 8), (1, 32)))
    up_weight = centred(splits[3], (D, FF), D ** -0.5, 0.078125, ((0, 8), (1, 32)))
    down_weight = centred(splits[4], (FF, D), FF ** -0.5, 0.0390625, ((0, 32), (1, 8)))
    return {"tokens": tokens, "cotangent": cotangent, "gate_weight": gate_weight, "up_weight": up_weight, "down_weight": down_weight}


def reference(tokens, cotangent, gate_weight, up_weight, down_weight):
    gate_value = jnp.dot(tokens, gate_weight, preferred_element_type=jnp.float32)
    up_value = jnp.dot(tokens, up_weight, preferred_element_type=jnp.float32)
    sigmoid_gate = jax.nn.sigmoid(gate_value)
    activated = gate_value * sigmoid_gate
    hidden = (activated * up_value).astype(jnp.bfloat16)
    output = jnp.dot(hidden, down_weight, preferred_element_type=jnp.float32).astype(jnp.bfloat16)
    slope_value = jnp.dot(cotangent, down_weight.T, preferred_element_type=jnp.float32)
    gate_slope = (slope_value * up_value * sigmoid_gate * (1.0 + gate_value * (1.0 - sigmoid_gate))).astype(jnp.bfloat16)
    up_slope = (slope_value * activated).astype(jnp.bfloat16)
    grad_tokens = (jnp.dot(gate_slope, gate_weight.T, preferred_element_type=jnp.float32)
                   + jnp.dot(up_slope, up_weight.T, preferred_element_type=jnp.float32)).astype(jnp.bfloat16)
    grad_scale = TOKENS ** -0.5
    grad_gate = (jnp.dot(tokens.T, gate_slope, preferred_element_type=jnp.float32) * grad_scale).astype(jnp.bfloat16)
    grad_up = (jnp.dot(tokens.T, up_slope, preferred_element_type=jnp.float32) * grad_scale).astype(jnp.bfloat16)
    grad_down = (jnp.dot(hidden.T, cotangent, preferred_element_type=jnp.float32) * grad_scale).astype(jnp.bfloat16)
    return output, grad_tokens, grad_gate, grad_up, grad_down
```

```python
import functools

import jax
import jax.numpy as jnp
from jax import lax
from jax.experimental import pallas as pl
from jax.experimental.pallas import tpu as pltpu
from jax.sharding import PartitionSpec as P

F32 = jnp.float32
BF16 = jnp.bfloat16
W = 768
HALF = W // 2
CHUNKS = 3
T = W // CHUNKS
PIECE = T // 4
ROWS = T // 16
LOCAL = 24

ZL, X1, C1, X2, C2, CORE, ZA, ZB, ZC, GN, GP, GF, GC, O1, G1, O2, G2, FIN = (
    0, 1, 4, 7, 10, 13, 16, 17, 18, 19, 20, 21, 22, 26, 29, 32, 35, 38)
COPIES = 39


def nt(a, b):
    return lax.dot_general(a, b, (((1,), (1,)), ((), ())), preferred_element_type=F32)


def nn(a, b):
    return jnp.dot(a, b, preferred_element_type=F32)


def tn(a, b):
    return lax.dot_general(a, b, (((0,), (0,)), ((), ())), preferred_element_type=F32)


def kernel(x_in, c_in, wg_hbm, wu_hbm, wd_hbm,
           out_ref, gt_ref, gg_hbm, gu_hbm, gd_hbm,
           wg, wu, wd, zsrc, zdst, xc, csnd, crcv, part, zsnd, zrcv, hid,
           pf, psnd, pown, p1rcv, sf, s1snd, s1own, p2rcv, fin, frcv, res,
           grads, ssem, rsem, lsem, gsem):
    depth, row, xx = lax.axis_index("depth"), lax.axis_index("row"), lax.axis_index("col")
    zl, y, zh, a = depth // 4, depth % 4, row // 2, row % 2
    nxt, prv, opp = (zh + 1 + 2 * a) % 4, (zh + 3 + 2 * a) % 4, (zh + 2) % 4

    def dev(zl_=zl, y_=y, zh_=zh, a_=a, x_=xx):
        return (zl_ * 4 + y_, zh_ * 2 + a_, x_)

    others = ([dev(zl_=1 - zl), dev(a_=1 - a), dev(zh_=nxt), dev(zh_=prv)]
              + [dev(x_=(xx + j) % 4) for j in (1, 2, 3)]
              + [dev(y_=(y + j) % 4) for j in (1, 2, 3)])
    mine = pl.ds(pl.multiple_of(a * HALF, 128), HALF)
    theirs = pl.ds(pl.multiple_of((1 - a) * HALF, 128), HALF)
    copies = {}

    def send(i, k, src, dst, to):
        copies[i, k] = pltpu.make_async_remote_copy(
            src_ref=src, dst_ref=dst, send_sem=ssem.at[i * COPIES + k],
            recv_sem=rsem.at[i * COPIES + k], device_id=to,
            device_id_type=pl.DeviceIdType.MESH)
        copies[i, k].start()

    def got(i, k, n=1):
        for j in range(n):
            copies[i, k + j].wait_recv()

    loads = [pltpu.make_async_copy(s, d, lsem.at[j])
             for j, (s, d) in enumerate(((wg_hbm, wg), (wu_hbm, wu), (wd_hbm, wd)))]
    for ld in loads:
        ld.start()
    barrier = pltpu.get_barrier_semaphore()
    for o in others:
        pl.semaphore_signal(barrier, inc=1, device_id=o, device_id_type=pl.DeviceIdType.MESH)
    for k, ref in enumerate((x_in, c_in)):
        v = ref[...].astype(F32)
        for i in range(CHUNKS):
            zsrc[i, k] = v[8 * i:8 * i + 8]
    pl.semaphore_wait(barrier, len(others))

    def zl_send(i):
        send(i, ZL, zsrc.at[i], zdst.at[i], dev(zl_=1 - zl))

    def ag1(i):
        got(i, ZL)
        for k in range(2):
            own, oth = zsrc[i, k], zdst[i, k]
            lo = jnp.where(zl == 0, own, oth)
            hi = jnp.where(zl == 0, oth, own)
            xc[i, k, y, xx] = jnp.concatenate([lo, hi], axis=0).astype(BF16)
        for j in (1, 2, 3):
            blk = xc.at[i, 0, y, xx]
            send(i, X1 + j - 1, blk, blk, dev(x_=(xx + j) % 4))
            blk = xc.at[i, 1, y, xx]
            send(i, C1 + j - 1, blk, blk, dev(y_=(y + j) % 4))

    def ag2(i):
        got(i, X1, 3)
        for j in (1, 2, 3):
            blk = xc.at[i, 0, y]
            send(i, X2 + j - 1, blk, blk, dev(y_=(y + j) % 4))
        got(i, C1, 3)
        for j in (1, 2, 3):
            blk = xc.at[i, 1, :, xx]
            send(i, C2 + j - 1, blk, blk, dev(x_=(xx + j) % 4))

    def mm(i):
        got(i, X2, 3)
        xs = xc[i, 0].reshape(T, W)
        csnd[i, 0] = nn(xs, wg[:, theirs])
        send(i, CORE, csnd.at[i, 0], crcv.at[i, 0], dev(a_=1 - a))
        csnd[i, 1] = nn(xs, wu[:, theirs])
        send(i, CORE + 1, csnd.at[i, 1], crcv.at[i, 1], dev(a_=1 - a))
        got(i, C2, 3)
        cs = xc[i, 1].reshape(T, W)
        csnd[i, 2] = nt(cs, wd[theirs, :])
        send(i, CORE + 2, csnd.at[i, 2], crcv.at[i, 2], dev(a_=1 - a))
        part[i, 0] = nn(xs, wg[:, mine]).reshape(4, PIECE, HALF)
        part[i, 1] = nn(xs, wu[:, mine]).reshape(4, PIECE, HALF)
        part[i, 2] = nt(cs, wd[mine, :]).reshape(4, PIECE, HALF)

    def rs1(i):
        got(i, CORE, 3)
        for j in range(3):
            part[i, j] = part[i, j] + crcv[i, j].reshape(4, PIECE, HALF)
        zsnd[i, 0] = part[i, :, opp].astype(BF16)
        send(i, ZA, zsnd.at[i, 0], zrcv.at[i, 0], dev(zh_=nxt))
        zsnd[i, 1] = part[i, :, prv].astype(BF16)
        send(i, ZB, zsnd.at[i, 1], zrcv.at[i, 1], dev(zh_=prv))

    def rs2(i):
        got(i, ZA)
        zsnd[i, 2] = (part[i, :, nxt] + zrcv[i, 0].astype(F32)).astype(BF16)
        send(i, ZC, zsnd.at[i, 2], zrcv.at[i, 2], dev(zh_=nxt))

    def el(i):
        got(i, ZB)
        got(i, ZC)
        tot = part[i, :, zh] + zrcv[i, 1].astype(F32) + zrcv[i, 2].astype(F32)
        gate, up, slope = tot[0], tot[1], tot[2]
        sig = 1.0 / (1.0 + jnp.exp(-gate))
        act = gate * sig
        hid[i, 0, zh, :, mine] = (act * up).astype(BF16)
        hid[i, 1, zh, :, mine] = (slope * up * sig * (1.0 + gate * (1.0 - sig))).astype(BF16)
        hid[i, 2, zh, :, mine] = (slope * act).astype(BF16)
        blk = hid.at[i, :, zh, :, mine]
        send(i, GN, blk, blk, dev(zh_=nxt))
        send(i, GP, blk, blk, dev(zh_=prv))
        send(i, GC, blk, blk, dev(a_=1 - a))

    def fw(i):
        got(i, GN)
        blk = hid.at[i, :, prv, :, mine]
        send(i, GF, blk, blk, dev(zh_=nxt))
        send(i, GC + 1, blk, blk, dev(a_=1 - a))
        got(i, GP)
        blk = hid.at[i, :, nxt, :, mine]
        send(i, GC + 2, blk, blk, dev(a_=1 - a))

    def fw2(i):
        got(i, GF)
        blk = hid.at[i, :, opp, :, mine]
        send(i, GC + 3, blk, blk, dev(a_=1 - a))

    def out(i):
        got(i, GC, 4)
        h = [hid[i, j].reshape(T, W) for j in range(3)]

        def cols_out(n, _):
            ds = pl.ds(pl.multiple_of(n * 256, 256), 256)
            p = nn(h[0], wd[:, ds]).reshape(4, 4, ROWS, 256)
            pf[0, :, :, :, ds] = p
            psnd[i, 0, :, :, :, ds] = p.astype(BF16)
            return _

        def cols_gt(n, _):
            ds = pl.ds(pl.multiple_of(n * 256, 256), 256)
            p = (nt(h[1], wg[ds, :]) + nt(h[2], wu[ds, :])).reshape(4, 4, ROWS, 256)
            pf[1, :, :, :, ds] = p
            psnd[i, 1, :, :, :, ds] = p.astype(BF16)
            return _

        lax.fori_loop(0, 3, cols_out, 0)
        for j in (1, 2, 3):
            to = (xx + j) % 4
            send(i, O1 + j - 1, psnd.at[i, 0, :, to], p1rcv.at[i, 0, j - 1], dev(x_=to))
        lax.fori_loop(0, 3, cols_gt, 0)
        for j in (1, 2, 3):
            to = (y + j) % 4
            send(i, G1 + j - 1, psnd.at[i, 1, to], p1rcv.at[i, 1, j - 1], dev(y_=to))
        pown[i, 0] = pf[0, :, xx]
        pown[i, 1] = pf[1, y]

    def o2(i):
        for k, (first, second) in enumerate(((O1, O2), (G1, G2))):
            got(i, first, 3)
            t = pown[i, k]
            for j in range(3):
                t = t + p1rcv[i, k, j].astype(F32)
            sf[...] = t
            s1snd[i, k] = t.astype(BF16)
            for j in (1, 2, 3):
                if k == 0:
                    to = (y + j) % 4
                    where = dev(y_=to)
                else:
                    to = (xx + j) % 4
                    where = dev(x_=to)
                send(i, second + j - 1, s1snd.at[i, k, to], p2rcv.at[i, k, j - 1], where)
            s1own[i, k] = sf[y] if k == 0 else sf[xx]

    def o3(i):
        for k, second in enumerate((O2, G2)):
            got(i, second, 3)
            t = s1own[i, k]
            for j in range(3):
                t = t + p2rcv[i, k, j].astype(F32)
            fin[i, k] = t.reshape(2, 8, W)
        send(i, FIN, fin.at[i, :, 1 - zl], frcv.at[i], dev(zl_=1 - zl))

    def o4(i):
        got(i, FIN)
        for k in range(2):
            res[k, 8 * i:8 * i + 8] = fin[i, k, zl] + frcv[i, k]

    scale = W ** -0.5
    stores = []

    def grad(which):
        src, k, hbm = ((0, 1, gg_hbm), (0, 2, gu_hbm), (1, 0, gd_hbm))[which]

        def rows(n, _):
            ds = pl.ds(pl.multiple_of(n * 256, 256), 256)
            if which < 2:
                lhs = xc[:, 0, :, :, :, ds].reshape(W, 256)
                rhs = hid[:, k].reshape(W, W)
            else:
                lhs = hid[:, 0, :, :, ds].reshape(W, 256)
                rhs = xc[:, 1].reshape(W, W)
            grads[which, ds, :] = (tn(lhs, rhs) * scale).astype(BF16)
            return _

        lax.fori_loop(0, 3, rows, 0)
        st = pltpu.make_async_copy(grads.at[which], hbm, gsem.at[which])
        st.start()
        stores.append(st)

    for i in range(CHUNKS):
        zl_send(i)
    ag1(0)
    ag2(0)
    ag1(1)
    for ld in loads:
        ld.wait()
    mm(0)
    rs1(0)
    ag2(1)
    ag1(2)
    rs2(0)
    mm(1)
    rs1(1)
    ag2(2)
    el(0)
    rs2(1)
    mm(2)
    rs1(2)
    fw(0)
    el(1)
    rs2(2)
    fw2(0)
    out(0)
    fw(1)
    el(2)
    o2(0)
    fw2(1)
    o3(0)
    out(1)
    fw(2)
    o4(0)
    o2(1)
    fw2(2)
    o3(1)
    out(2)
    grad(0)
    o4(1)
    grad(1)
    o2(2)
    grad(2)
    o3(2)
    o4(2)
    out_ref[...] = res[0].astype(BF16)
    gt_ref[...] = res[1].astype(BF16)
    for c in copies.values():
        c.wait_send()
    for st in stores:
        st.wait()


def local(tokens, cotangent, gate_weight, up_weight, down_weight):
    vmem = pl.BlockSpec(memory_space=pltpu.VMEM)
    hbm = pl.BlockSpec(memory_space=pl.ANY)
    small = jax.ShapeDtypeStruct((LOCAL, W), BF16)
    big = jax.ShapeDtypeStruct((W, W), BF16)
    return pl.pallas_call(
        kernel,
        name="swiglu",
        out_shape=(small, small, big, big, big),
        in_specs=[vmem, vmem, hbm, hbm, hbm],
        out_specs=(vmem, vmem, hbm, hbm, hbm),
        scratch_shapes=[
            pltpu.VMEM((W, W), BF16),
            pltpu.VMEM((W, W), BF16),
            pltpu.VMEM((W, W), BF16),
            pltpu.VMEM((CHUNKS, 2, 8, W), F32),
            pltpu.VMEM((CHUNKS, 2, 8, W), F32),
            pltpu.VMEM((CHUNKS, 2, 4, 4, ROWS, W), BF16),
            pltpu.VMEM((CHUNKS, 3, T, HALF), F32),
            pltpu.VMEM((CHUNKS, 3, T, HALF), F32),
            pltpu.VMEM((CHUNKS, 3, 4, PIECE, HALF), F32),
            pltpu.VMEM((CHUNKS, 3, 3, PIECE, HALF), BF16),
            pltpu.VMEM((CHUNKS, 3, 3, PIECE, HALF), BF16),
            pltpu.VMEM((CHUNKS, 3, 4, PIECE, W), BF16),
            pltpu.VMEM((2, 4, 4, ROWS, W), F32),
            pltpu.VMEM((CHUNKS, 2, 4, 4, ROWS, W), BF16),
            pltpu.VMEM((CHUNKS, 2, 4, ROWS, W), F32),
            pltpu.VMEM((CHUNKS, 2, 3, 4, ROWS, W), BF16),
            pltpu.VMEM((4, ROWS, W), F32),
            pltpu.VMEM((CHUNKS, 2, 4, ROWS, W), BF16),
            pltpu.VMEM((CHUNKS, 2, ROWS, W), F32),
            pltpu.VMEM((CHUNKS, 2, 3, ROWS, W), BF16),
            pltpu.VMEM((CHUNKS, 2, 2, 8, W), F32),
            pltpu.VMEM((CHUNKS, 2, 8, W), F32),
            pltpu.VMEM((2, LOCAL, W), F32),
            pltpu.VMEM((3, W, W), BF16),
            pltpu.SemaphoreType.DMA((CHUNKS * COPIES,)),
            pltpu.SemaphoreType.DMA((CHUNKS * COPIES,)),
            pltpu.SemaphoreType.DMA((3,)),
            pltpu.SemaphoreType.DMA((3,)),
        ],
        compiler_params=pltpu.CompilerParams(
            collective_id=0, has_side_effects=True, vmem_limit_bytes=60 << 20),
        cost_estimate=pl.CostEstimate(
            flops=18 * W ** 3, bytes_accessed=12 * W * W, transcendentals=W * W // 8),
    )(tokens, cotangent, gate_weight, up_weight, down_weight)


def solution(mesh):
    by_token = P(("depth", "col"), "row")
    by_model = P("row", ("depth", "col"))
    return jax.shard_map(
        local,
        mesh=mesh,
        in_specs=(by_token, by_token, by_model, by_model, by_token),
        out_specs=(by_token, by_token, by_model, by_model, by_token),
        check_vma=False,
    )
```

```python
import functools

import jax
import jax.numpy as jnp
from jax import lax
from jax.experimental import pallas as pl
from jax.experimental.pallas import tpu as pltpu
from jax.sharding import PartitionSpec as P

F32 = jnp.float32
BF16 = jnp.bfloat16
W = 768
HALF = W // 2
LOCAL = 24
UNIT = 128

SIZES = (1, 1, 2, 1, 1)
OWN = (0, 4, 5)
OTHER = (1, 2, 3)

X1, C1, X2, C2, CORE, ZA, ZB, ZC, GN, GP, GF, GC, O1, G1, O2, G2 = (
    0, 3, 6, 9, 12, 15, 16, 17, 18, 19, 20, 21, 25, 28, 31, 34)
COPIES = 37
ZL, FIN = 0, 3
SEMS = COPIES * len(SIZES) + 4

PLAN = (
    ("zl_send", 0), ("zl_send", 1), ("zl_send", 2), ("ready", 0), ("ag1", 0), ("ag1", 1),
    ("ag2", 0), ("ag1", 2), ("ag1", 3), ("ag1", 4), ("ag2", 1), ("mm", 0),
    ("ag2", 2), ("ag2", 3), ("ag2", 4), ("rs1", 0), ("mm", 1), ("rs2", 0),
    ("rs1", 1), ("mm", 2), ("el", 0), ("mm", 3), ("rs2", 1), ("mm", 4),
    ("fw", 0), ("rs1", 2), ("fp", 0), ("el", 1), ("fw2", 0), ("out", 0),
    ("rs2", 2), ("o2", 0), ("o3", 0), ("sent", 0), ("fw", 1), ("rs1", 3),
    ("fp", 1), ("el", 2), ("fw2", 1), ("out", 1), ("rs2", 3), ("o2", 1),
    ("fw", 2), ("rs1", 4), ("o3", 1), ("sent", 1), ("fp", 2), ("el", 3),
    ("fw2", 2), ("out", 2), ("rs2", 4), ("fw", 3), ("fp", 3), ("el", 4),
    ("o2", 2), ("fw2", 3), ("out", 3), ("fw", 4), ("o3", 2), ("sent", 2),
    ("fp", 4), ("o2", 3), ("fw2", 4), ("fin_send", 0), ("out", 4), ("o3", 3),
    ("grad", 0), ("grad", 1), ("grad", 2), ("o2", 4), ("sent", 3), ("o3", 4),
    ("sent", 4), ("end", 0),
)


def nt(a, b):
    return lax.dot_general(a, b, (((1,), (1,)), ((), ())), preferred_element_type=F32)


def nn(a, b):
    return jnp.dot(a, b, preferred_element_type=F32)


def tn(a, b):
    return lax.dot_general(a, b, (((0,), (0,)), ((), ())), preferred_element_type=F32)


def fold(v):
    v = v.reshape(v.shape[0] // 8, 8, W)
    return jnp.concatenate([v[:, :, :HALF], v[:, :, HALF:]], axis=1)


def unfold(v):
    v = jnp.concatenate([v[:, :8], v[:, 8:]], axis=2)
    return v.reshape(v.shape[0] * 8, W)


def kernel(plan, x_in, c_in, wg_hbm, wu_hbm, wd_hbm,
           out_ref, gt_ref, gg_hbm, gu_hbm, gd_hbm,
           wg, wu, wd, xc, xg, csnd, crcv, part, zsnd, zrcv, hid,
           pf, psnd, p1rcv, sf, s1snd, s1own, p2rcv, fin, frcv,
           grads, ssem, rsem, lsem, gsem):
    depth, row, xx = lax.axis_index("depth"), lax.axis_index("row"), lax.axis_index("col")
    zl, y, zh, a = depth // 4, depth % 4, row // 2, row % 2
    nxt, prv, opp = (zh + 1 + 2 * a) % 4, (zh + 3 + 2 * a) % 4, (zh + 2) % 4

    def dev(zl_=zl, y_=y, zh_=zh, a_=a, x_=xx):
        return (zl_ * 4 + y_, zh_ * 2 + a_, x_)

    others = ([dev(zl_=1 - zl), dev(a_=1 - a), dev(zh_=nxt), dev(zh_=prv)]
              + [dev(x_=(xx + j) % 4) for j in (1, 2, 3)]
              + [dev(y_=(y + j) % 4) for j in (1, 2, 3)])
    mine = pl.ds(pl.multiple_of(a * HALF, 128), HALF)
    theirs = pl.ds(pl.multiple_of((1 - a) * HALF, 128), HALF)
    copies = {}

    def units(i):
        return slice(sum(SIZES[:i]), sum(SIZES[:i + 1]))

    def rows(i):
        return slice(UNIT * sum(SIZES[:i]), UNIT * sum(SIZES[:i + 1]))

    def quarter(i):
        return slice(UNIT // 4 * sum(SIZES[:i]), UNIT // 4 * sum(SIZES[:i + 1]))

    def piece(i, q):
        n = UNIT // 4 * SIZES[i]
        return pl.ds(pl.multiple_of(UNIT * sum(SIZES[:i]) + n * q, 32), n)

    def send(i, k, src, dst, to):
        s = COPIES * i + k
        copies[i, k] = pltpu.make_async_remote_copy(
            src_ref=src, dst_ref=dst, send_sem=ssem.at[s], recv_sem=rsem.at[s],
            device_id=to, device_id_type=pl.DeviceIdType.MESH)
        copies[i, k].start()

    def got(i, k, n=1):
        for j in range(n):
            copies[i, k + j].wait_recv()

    glob = len(SIZES)

    loads = [pltpu.make_async_copy(s, d, lsem.at[j])
             for j, (s, d) in enumerate(((wg_hbm, wg), (wu_hbm, wu), (wd_hbm, wd)))]
    for ld in loads:
        ld.start()
    barrier = pltpu.get_barrier_semaphore()
    for o in others:
        pl.semaphore_signal(barrier, inc=1, device_id=o, device_id_type=pl.DeviceIdType.MESH)
    for k, ref in enumerate((x_in, c_in)):
        v = fold(ref[...].astype(F32)).astype(BF16)
        for u in range(3):
            xc[k, OWN[u], y, xx] = v[u]
    pl.semaphore_wait(barrier, len(others))

    def zl_send(u):
        send(glob, ZL + u, xc.at[:, OWN[u], y, xx], xc.at[:, OTHER[u], y, xx], dev(zl_=1 - zl))

    def ag1(i):
        es = units(i)
        for e in range(es.start, es.stop):
            if e in OTHER:
                got(glob, ZL + OTHER.index(e))
        for j in (1, 2, 3):
            blk = xc.at[0, es, y, xx]
            send(i, X1 + j - 1, blk, blk, dev(x_=(xx + j) % 4))
            blk = xc.at[1, es, y, xx]
            send(i, C1 + j - 1, blk, blk, dev(y_=(y + j) % 4))

    def ag2(i):
        es = units(i)
        got(i, X1, 3)
        for j in (1, 2, 3):
            blk = xc.at[0, es, y]
            send(i, X2 + j - 1, blk, blk, dev(y_=(y + j) % 4))
        got(i, C1, 3)
        for j in (1, 2, 3):
            blk = xc.at[1, es, :, xx]
            send(i, C2 + j - 1, blk, blk, dev(x_=(xx + j) % 4))

    def ready(_):
        for ld in loads:
            ld.wait()

    def gathered(i, k):
        v = xc[k, units(i)].reshape(16 * SIZES[i], 16, HALF)
        v = unfold(v.astype(F32)).astype(BF16)
        xg[k, rows(i)] = v
        return v

    def mm(i):
        rs = rows(i)
        got(i, X2, 3)
        xs = gathered(i, 0)
        csnd[0, rs] = nn(xs, wg[:, theirs])
        send(i, CORE, csnd.at[0, rs], crcv.at[0, rs], dev(a_=1 - a))
        csnd[1, rs] = nn(xs, wu[:, theirs])
        send(i, CORE + 1, csnd.at[1, rs], crcv.at[1, rs], dev(a_=1 - a))
        got(i, C2, 3)
        cs = gathered(i, 1)
        csnd[2, rs] = nt(cs, wd[theirs, :])
        send(i, CORE + 2, csnd.at[2, rs], crcv.at[2, rs], dev(a_=1 - a))
        part[0, rs] = nn(xs, wg[:, mine])
        part[1, rs] = nn(xs, wu[:, mine])
        part[2, rs] = nt(cs, wd[mine, :])

    def rs1(i):
        rs, qs = rows(i), quarter(i)
        got(i, CORE, 3)
        part[:, rs] = part[:, rs] + crcv[:, rs]
        zsnd[0, :, qs] = part[:, piece(i, opp)].astype(BF16)
        send(i, ZA, zsnd.at[0, :, qs], zrcv.at[0, :, qs], dev(zh_=nxt))
        zsnd[1, :, qs] = part[:, piece(i, prv)].astype(BF16)
        send(i, ZB, zsnd.at[1, :, qs], zrcv.at[1, :, qs], dev(zh_=prv))

    def rs2(i):
        qs = quarter(i)
        got(i, ZA)
        zsnd[2, :, qs] = (part[:, piece(i, nxt)] + zrcv[0, :, qs].astype(F32)).astype(BF16)
        send(i, ZC, zsnd.at[2, :, qs], zrcv.at[2, :, qs], dev(zh_=nxt))

    def el(i):
        qs, ps = quarter(i), piece(i, zh)
        got(i, ZB)
        got(i, ZC)
        tot = part[:, ps] + zrcv[1, :, qs].astype(F32) + zrcv[2, :, qs].astype(F32)
        gate, up, slope = tot[0], tot[1], tot[2]
        sig = 1.0 / (1.0 + jnp.exp(-gate))
        act = gate * sig
        hid[0, ps, mine] = (act * up).astype(BF16)
        hid[1, ps, mine] = (slope * up * sig * (1.0 + gate * (1.0 - sig))).astype(BF16)
        hid[2, ps, mine] = (slope * act).astype(BF16)
        blk = hid.at[:, ps, mine]
        send(i, GN, blk, blk, dev(zh_=nxt))
        send(i, GP, blk, blk, dev(zh_=prv))
        send(i, GC, blk, blk, dev(a_=1 - a))

    def fw(i):
        got(i, GN)
        blk = hid.at[:, piece(i, prv), mine]
        send(i, GF, blk, blk, dev(zh_=nxt))
        send(i, GC + 1, blk, blk, dev(a_=1 - a))

    def fp(i):
        got(i, GP)
        blk = hid.at[:, piece(i, nxt), mine]
        send(i, GC + 2, blk, blk, dev(a_=1 - a))

    def fw2(i):
        got(i, GF)
        blk = hid.at[:, piece(i, opp), mine]
        send(i, GC + 3, blk, blk, dev(a_=1 - a))

    def out(i):
        rs, es, n = rows(i), units(i), SIZES[i]
        got(i, GC, 4)
        p = fold(nn(hid[0, rs], wd[...])).reshape(n, 4, 4, 16, HALF)
        pf[0, es] = p
        psnd[0, es] = p.astype(BF16)
        for j in (1, 2, 3):
            to = (xx + j) % 4
            send(i, O1 + j - 1, psnd.at[0, es, :, to], p1rcv.at[0, j - 1, es], dev(x_=to))
        p = fold(nt(hid[1, rs], wg[...]) + nt(hid[2, rs], wu[...])).reshape(n, 4, 4, 16, HALF)
        pf[1, es] = p
        psnd[1, es] = p.astype(BF16)
        for j in (1, 2, 3):
            to = (y + j) % 4
            send(i, G1 + j - 1, psnd.at[1, es, to], p1rcv.at[1, j - 1, es], dev(y_=to))

    def o2(i):
        es = units(i)
        for k, (first, second) in enumerate(((O1, O2), (G1, G2))):
            got(i, first, 3)
            t = pf[0, es, :, xx] if k == 0 else pf[1, es, y]
            for j in range(3):
                t = t + p1rcv[k, j, es].astype(F32)
            sf[:SIZES[i]] = t
            s1snd[k, es] = t.astype(BF16)
            for j in (1, 2, 3):
                if k == 0:
                    to = (y + j) % 4
                    where = dev(y_=to)
                else:
                    to = (xx + j) % 4
                    where = dev(x_=to)
                send(i, second + j - 1, s1snd.at[k, es, to], p2rcv.at[k, j - 1, es], where)
            s1own[k, es] = sf[:SIZES[i], y] if k == 0 else sf[:SIZES[i], xx]

    def o3(i):
        es = units(i)
        for k, second in enumerate((O2, G2)):
            got(i, second, 3)
            t = s1own[k, es]
            for j in range(3):
                t = t + p2rcv[k, j, es].astype(F32)
            fin[k, es] = t

    def fin_send(_):
        send(glob, FIN, fin.at[:, OTHER[0]:OTHER[-1] + 1], frcv, dev(zl_=1 - zl))

    def sent(i):
        for k in range(COPIES):
            copies[i, k].wait_send()

    scale = W ** -0.5
    stores = []

    def grad(which):
        lhs, k, hbm = ((xg.at[0], 1, gg_hbm), (xg.at[0], 2, gu_hbm), (hid.at[0], 0, gd_hbm))[which]

        def tile(n, _):
            ds = pl.ds(pl.multiple_of(n * 256, 256), 256)
            rhs = hid[k] if which < 2 else xg[1]
            grads[which, ds, :] = (tn(lhs[:, ds], rhs) * scale).astype(BF16)
            return _

        lax.fori_loop(0, 3, tile, 0)
        st = pltpu.make_async_copy(grads.at[which], hbm, gsem.at[which])
        st.start()
        stores.append(st)

    def end(_):
        got(glob, FIN)
        for k, ref in enumerate((out_ref, gt_ref)):
            v = jnp.stack([fin[k, e] for e in OWN]) + frcv[k]
            ref[...] = unfold(v).astype(BF16)

    steps = {f.__name__: f for f in (zl_send, ag1, ag2, ready, mm, rs1, rs2, el, fw, fp, fw2,
                                     out, o2, o3, fin_send, sent, grad, end)}
    for name, i in plan:
        steps[name](i)
    for st in stores:
        st.wait()
    for k in (ZL, ZL + 1, ZL + 2, FIN):
        copies[glob, k].wait_send()


def move(a, b, c, d, e, a_out, b_out, c_out, d_out, e_out, sem):
    pairs = ((c, c_out), (d, d_out), (e, e_out), (a, a_out), (b, b_out))
    moves = [pltpu.make_async_copy(s, t, sem.at[j]) for j, (s, t) in enumerate(pairs)]
    for m in moves:
        m.start()
    for m in moves:
        m.wait()


def local(tokens, cotangent, gate_weight, up_weight, down_weight):
    vmem = pl.BlockSpec(memory_space=pltpu.VMEM)
    hbm = pl.BlockSpec(memory_space=pl.ANY)
    small = jax.ShapeDtypeStruct((LOCAL, W), BF16)
    big = jax.ShapeDtypeStruct((W, W), BF16)
    results = pl.pallas_call(
        functools.partial(kernel, PLAN),
        name="swiglu",
        out_shape=(small, small, big, big, big),
        in_specs=[vmem, vmem, hbm, hbm, hbm],
        out_specs=(vmem, vmem, hbm, hbm, hbm),
        scratch_shapes=[
            pltpu.VMEM((W, W), BF16),
            pltpu.VMEM((W, W), BF16),
            pltpu.VMEM((W, W), BF16),
            pltpu.VMEM((2, 6, 4, 4, 16, HALF), BF16),
            pltpu.VMEM((2, W, W), BF16),
            pltpu.VMEM((3, W, HALF), F32),
            pltpu.VMEM((3, W, HALF), F32),
            pltpu.VMEM((3, W, HALF), F32),
            pltpu.VMEM((3, 3, W // 4, HALF), BF16),
            pltpu.VMEM((3, 3, W // 4, HALF), BF16),
            pltpu.VMEM((3, W, W), BF16),
            pltpu.VMEM((2, 6, 4, 4, 16, HALF), F32),
            pltpu.VMEM((2, 6, 4, 4, 16, HALF), BF16),
            pltpu.VMEM((2, 3, 6, 4, 16, HALF), BF16),
            pltpu.VMEM((max(SIZES), 4, 16, HALF), F32),
            pltpu.VMEM((2, 6, 4, 16, HALF), BF16),
            pltpu.VMEM((2, 6, 16, HALF), F32),
            pltpu.VMEM((2, 3, 6, 16, HALF), BF16),
            pltpu.VMEM((2, 6, 16, HALF), F32),
            pltpu.VMEM((2, 3, 16, HALF), F32),
            pltpu.VMEM((3, W, W), BF16),
            pltpu.SemaphoreType.DMA((SEMS,)),
            pltpu.SemaphoreType.DMA((SEMS,)),
            pltpu.SemaphoreType.DMA((3,)),
            pltpu.SemaphoreType.DMA((3,)),
        ],
        compiler_params=pltpu.CompilerParams(
            collective_id=0, has_side_effects=True, vmem_limit_bytes=56 << 20),
        cost_estimate=pl.CostEstimate(
            flops=18 * W ** 3, bytes_accessed=12 * W * W, transcendentals=W * W // 8),
    )(tokens, cotangent, gate_weight, up_weight, down_weight)
    return pl.pallas_call(
        move,
        name="move",
        out_shape=(small, small, big, big, big),
        in_specs=[hbm] * 5,
        out_specs=(hbm,) * 5,
        scratch_shapes=[pltpu.SemaphoreType.DMA((5,))],
    )(*results)


def solution(mesh):
    by_token = P(("depth", "col"), "row")
    by_model = P("row", ("depth", "col"))
    return jax.shard_map(
        local,
        mesh=mesh,
        in_specs=(by_token, by_token, by_model, by_model, by_token),
        out_specs=(by_token, by_token, by_model, by_model, by_token),
        check_vma=False,
    )
```

```python
import functools

import jax
import jax.numpy as jnp
from jax import lax
from jax.experimental import pallas as pl
from jax.experimental.pallas import tpu as pltpu
from jax.sharding import PartitionSpec as P

F32 = jnp.float32
BF16 = jnp.bfloat16
W = 768
HALF = W // 2
LOCAL = 24
UNIT = 128

SIZES = (1, 1, 2, 1, 1)
OWN = (0, 4, 5)
OTHER = (1, 2, 3)

X1, C1, X2, C2, CORE, ZA, ZB, ZC, GN, GP, GF, GC, O1, G1, O2, G2 = range(16)
KINDS = 16
ZL, FIN = 0, 3
SENDS = KINDS + 2
RECVS = KINDS * len(SIZES) + 4

PLAN = (
    ("ag1", 3), ("ag1", 0), ("ready", 0), ("ag1", 4), ("zl_send", 0), ("zl_send", 2),
    ("ag2c", 3), ("ag2x", 3), ("zl_send", 1), ("ag2x", 0), ("ag2c", 0), ("ag1", 1),
    ("mmc", 3), ("mmx", 3), ("mmx", 0), ("rs1", 3), ("ag1", 2), ("ag2x", 1),
    ("ag2c", 1), ("mmc", 0), ("rs1", 0), ("rs2", 3), ("ag2c", 4), ("mmc", 1),
    ("mmx", 1), ("ag2c", 2), ("ag2x", 2), ("rs2", 0), ("rs1", 1), ("el", 3),
    ("rs2", 1), ("el", 0), ("mmc", 2), ("ag2x", 4), ("mmx", 2), ("fw", 3),
    ("rs1", 2), ("fp", 3), ("fw2", 3), ("el", 1), ("outa", 3), ("fp", 0),
    ("mmc", 4), ("outb", 3), ("fw", 0), ("mmx", 4), ("rs2", 2), ("fp", 1),
    ("fw", 1), ("rs1", 4), ("fw2", 0), ("el", 2), ("fw2", 1), ("outa", 1),
    ("outa", 0), ("o2b", 3), ("rs2", 4), ("outb", 0), ("outb", 1), ("fw", 2),
    ("o2a", 1), ("el", 4), ("o3b", 3), ("fp", 2), ("fw2", 2), ("fw", 4),
    ("outa", 2), ("outb", 2), ("o2a", 0), ("o2b", 1), ("fp", 4), ("fw2", 4),
    ("outa", 4), ("o2a", 2), ("o3b", 1), ("o2a", 3), ("o2b", 2), ("outb", 4),
    ("grad", 2), ("o3a", 2), ("o2b", 0), ("o2a", 4), ("o3a", 1), ("o3b", 2),
    ("fin_send", 0), ("grad", 1), ("o2b", 4), ("grad", 0), ("o3b", 0), ("o3a", 3),
    ("o3a", 4), ("o3a", 0), ("o3b", 4), ("sent", 0), ("end", 0),
)


def nt(a, b):
    return lax.dot_general(a, b, (((1,), (1,)), ((), ())), preferred_element_type=F32)


def nn(a, b):
    return jnp.dot(a, b, preferred_element_type=F32)


def tn(a, b):
    return lax.dot_general(a, b, (((0,), (0,)), ((), ())), preferred_element_type=F32)


def fold(v):
    v = v.reshape(v.shape[0] // 8, 8, W)
    return jnp.concatenate([v[:, :, :HALF], v[:, :, HALF:]], axis=1)


def unfold(v):
    v = jnp.concatenate([v[:, :8], v[:, 8:]], axis=2)
    return v.reshape(v.shape[0] * 8, W)


def kernel(plan, x_in, c_in, wg_hbm, wu_hbm, wd_hbm,
           out_ref, gt_ref, gg_hbm, gu_hbm, gd_hbm,
           wg, wu, wd, xc, xg, csnd, crcv, part, zsnd, zrcv, hid,
           pf, psnd, p1rcv, sf, s1snd, s1own, p2rcv, fin, frcv,
           grads, ssem, rsem, lsem, gsem):
    depth, row, xx = lax.axis_index("depth"), lax.axis_index("row"), lax.axis_index("col")
    zl, y, zh, a = depth // 4, depth % 4, row // 2, row % 2
    nxt, prv, opp = (zh + 1 + 2 * a) % 4, (zh + 3 + 2 * a) % 4, (zh + 2) % 4

    def dev(zl_=zl, y_=y, zh_=zh, a_=a, x_=xx):
        return (zl_ * 4 + y_, zh_ * 2 + a_, x_)

    others = ([dev(zl_=1 - zl), dev(a_=1 - a), dev(zh_=nxt), dev(zh_=prv)]
              + [dev(x_=(xx + j) % 4) for j in (1, 2, 3)]
              + [dev(y_=(y + j) % 4) for j in (1, 2, 3)])
    mine = pl.ds(pl.multiple_of(a * HALF, 128), HALF)
    theirs = pl.ds(pl.multiple_of((1 - a) * HALF, 128), HALF)
    def units(i):
        return slice(sum(SIZES[:i]), sum(SIZES[:i + 1]))

    def rows(i):
        return slice(UNIT * sum(SIZES[:i]), UNIT * sum(SIZES[:i + 1]))

    def quarter(i):
        return slice(UNIT // 4 * sum(SIZES[:i]), UNIT // 4 * sum(SIZES[:i + 1]))

    def piece(i, q):
        n = UNIT // 4 * SIZES[i]
        return pl.ds(pl.multiple_of(UNIT * sum(SIZES[:i]) + n * q, 32), n)

    def push(ssem_at, rsem_at, src, dst, to):
        pltpu.make_async_remote_copy(
            src_ref=src, dst_ref=dst, send_sem=ssem.at[ssem_at], recv_sem=rsem.at[rsem_at],
            device_id=to, device_id_type=pl.DeviceIdType.MESH).start()

    def send(i, k, src, dst, to):
        push(k, KINDS * i + k, src, dst, to)

    def wait(sem, ref):
        pltpu.make_async_copy(ref, ref, sem).wait()

    def got(i, k, ref):
        wait(rsem.at[KINDS * i + k], ref)

    last = KINDS * len(SIZES)

    loads = [pltpu.make_async_copy(s, d, lsem.at[j])
             for j, (s, d) in enumerate(((wg_hbm, wg), (wu_hbm, wu), (wd_hbm, wd)))]
    for ld in loads:
        ld.start()
    barrier = pltpu.get_barrier_semaphore()
    for o in others:
        pl.semaphore_signal(barrier, inc=1, device_id=o, device_id_type=pl.DeviceIdType.MESH)
    for k, ref in enumerate((x_in, c_in)):
        v = fold(ref[...].astype(F32)).astype(BF16)
        for u in range(3):
            xc[k, OWN[u], y, xx] = v[u]
    pl.semaphore_wait(barrier, len(others))

    def zl_send(u):
        push(KINDS, last + ZL + u,
             xc.at[:, OWN[u], y, xx], xc.at[:, OTHER[u], y, xx], dev(zl_=1 - zl))

    def ag1(i):
        es = units(i)
        for e in range(es.start, es.stop):
            if e in OTHER:
                wait(rsem.at[last + ZL + OTHER.index(e)], xc.at[:, e, y, xx])
        for j in (1, 2, 3):
            blk = xc.at[0, es, y, xx]
            send(i, X1, blk, blk, dev(x_=(xx + j) % 4))
            blk = xc.at[1, es, y, xx]
            send(i, C1, blk, blk, dev(y_=(y + j) % 4))

    def ag2x(i):
        es = units(i)
        got(i, X1, xc.at[0, es, y, :3])
        for j in (1, 2, 3):
            blk = xc.at[0, es, y]
            send(i, X2, blk, blk, dev(y_=(y + j) % 4))

    def ag2c(i):
        es = units(i)
        got(i, C1, xc.at[1, es, :3, xx])
        for j in (1, 2, 3):
            blk = xc.at[1, es, :, xx]
            send(i, C2, blk, blk, dev(x_=(xx + j) % 4))

    def ready(_):
        for ld in loads:
            ld.wait()

    def gathered(i, k):
        v = xc[k, units(i)].reshape(16 * SIZES[i], 16, HALF)
        v = unfold(v.astype(F32)).astype(BF16)
        xg[k, rows(i)] = v
        return v

    def mmx(i):
        rs = rows(i)
        got(i, X2, xc.at[0, units(i), :3])
        xs = gathered(i, 0)
        for j, w in ((0, wg), (1, wu)):
            csnd[j, rs] = nn(xs, w[:, theirs])
            send(i, CORE, csnd.at[j, rs], crcv.at[j, rs], dev(a_=1 - a))
        part[0, rs] = nn(xs, wg[:, mine])
        part[1, rs] = nn(xs, wu[:, mine])

    def mmc(i):
        rs = rows(i)
        got(i, C2, xc.at[1, units(i), :3])
        cs = gathered(i, 1)
        csnd[2, rs] = nt(cs, wd[theirs, :])
        send(i, CORE, csnd.at[2, rs], crcv.at[2, rs], dev(a_=1 - a))
        part[2, rs] = nt(cs, wd[mine, :])

    def rs1(i):
        rs, qs = rows(i), quarter(i)
        got(i, CORE, crcv.at[:, rs])
        part[:, rs] = part[:, rs] + crcv[:, rs]
        zsnd[0, :, qs] = part[:, piece(i, opp)].astype(BF16)
        send(i, ZA, zsnd.at[0, :, qs], zrcv.at[0, :, qs], dev(zh_=nxt))
        zsnd[1, :, qs] = part[:, piece(i, prv)].astype(BF16)
        send(i, ZB, zsnd.at[1, :, qs], zrcv.at[1, :, qs], dev(zh_=prv))

    def rs2(i):
        qs = quarter(i)
        got(i, ZA, zrcv.at[0, :, qs])
        zsnd[2, :, qs] = (part[:, piece(i, nxt)] + zrcv[0, :, qs].astype(F32)).astype(BF16)
        send(i, ZC, zsnd.at[2, :, qs], zrcv.at[2, :, qs], dev(zh_=nxt))

    def el(i):
        qs, ps = quarter(i), piece(i, zh)
        got(i, ZB, zrcv.at[1, :, qs])
        got(i, ZC, zrcv.at[2, :, qs])
        tot = part[:, ps] + zrcv[1, :, qs].astype(F32) + zrcv[2, :, qs].astype(F32)
        gate, up, slope = tot[0], tot[1], tot[2]
        sig = 1.0 / (1.0 + jnp.exp(-gate))
        act = gate * sig
        hid[0, ps, mine] = (act * up).astype(BF16)
        hid[1, ps, mine] = (slope * up * sig * (1.0 + gate * (1.0 - sig))).astype(BF16)
        hid[2, ps, mine] = (slope * act).astype(BF16)
        blk = hid.at[:, ps, mine]
        send(i, GN, blk, blk, dev(zh_=nxt))
        send(i, GP, blk, blk, dev(zh_=prv))
        send(i, GC, blk, blk, dev(a_=1 - a))

    def fw(i):
        blk = hid.at[:, piece(i, prv), mine]
        got(i, GN, blk)
        send(i, GF, blk, blk, dev(zh_=nxt))
        send(i, GC, blk, blk, dev(a_=1 - a))

    def fp(i):
        blk = hid.at[:, piece(i, nxt), mine]
        got(i, GP, blk)
        send(i, GC, blk, blk, dev(a_=1 - a))

    def fw2(i):
        blk = hid.at[:, piece(i, opp), mine]
        got(i, GF, blk)
        send(i, GC, blk, blk, dev(a_=1 - a))

    def outa(i):
        rs, es, n = rows(i), units(i), SIZES[i]
        got(i, GC, hid.at[:, rs, theirs])
        p = fold(nn(hid[0, rs], wd[...])).reshape(n, 4, 4, 16, HALF)
        pf[0, es] = p
        psnd[0, es] = p.astype(BF16)
        for j in (1, 2, 3):
            to = (xx + j) % 4
            send(i, O1, psnd.at[0, es, :, to], p1rcv.at[0, j - 1, es], dev(x_=to))

    def outb(i):
        rs, es, n = rows(i), units(i), SIZES[i]
        p = fold(nt(hid[1, rs], wg[...]) + nt(hid[2, rs], wu[...])).reshape(n, 4, 4, 16, HALF)
        pf[1, es] = p
        psnd[1, es] = p.astype(BF16)
        for j in (1, 2, 3):
            to = (y + j) % 4
            send(i, G1, psnd.at[1, es, to], p1rcv.at[1, j - 1, es], dev(y_=to))

    def second(i, k, t):
        es = units(i)
        for j in range(3):
            t = t + p1rcv[k, j, es].astype(F32)
        sf[:SIZES[i]] = t
        s1snd[k, es] = t.astype(BF16)

    def o2a(i):
        es = units(i)
        got(i, O1, p1rcv.at[0, :, es])
        second(i, 0, pf[0, es, :, xx])
        for j in (1, 2, 3):
            to = (y + j) % 4
            send(i, O2, s1snd.at[0, es, to], p2rcv.at[0, j - 1, es], dev(y_=to))
        s1own[0, es] = sf[:SIZES[i], y]

    def o2b(i):
        es = units(i)
        got(i, G1, p1rcv.at[1, :, es])
        second(i, 1, pf[1, es, y])
        for j in (1, 2, 3):
            to = (xx + j) % 4
            send(i, G2, s1snd.at[1, es, to], p2rcv.at[1, j - 1, es], dev(x_=to))
        s1own[1, es] = sf[:SIZES[i], xx]

    def third(i, k, kind):
        es = units(i)
        got(i, kind, p2rcv.at[k, :, es])
        t = s1own[k, es]
        for j in range(3):
            t = t + p2rcv[k, j, es].astype(F32)
        fin[k, es] = t

    def o3a(i):
        third(i, 0, O2)

    def o3b(i):
        third(i, 1, G2)

    def fin_send(_):
        push(KINDS + 1, last + FIN, fin.at[:, OTHER[0]:OTHER[-1] + 1], frcv, dev(zl_=1 - zl))

    def sent(_):
        block, half = xc.at[0, :, 0, :3], hid.at[:, :, :HALF]
        for k, ref in ((X1, block), (C1, block), (X2, xc.at[0, :, :3]), (C2, xc.at[1, :, :3]),
                       (CORE, csnd), (ZA, zsnd.at[0]), (ZB, zsnd.at[1]), (ZC, zsnd.at[2]),
                       (GN, zsnd.at[0]), (GP, zsnd.at[1]), (GF, zsnd.at[2]), (GC, half),
                       (O1, p1rcv.at[0]), (G1, p1rcv.at[1]), (O2, p2rcv.at[0]),
                       (G2, p2rcv.at[1]), (KINDS, xc.at[:, :3, 0, 0]), (KINDS + 1, frcv)):
            wait(ssem.at[k], ref)

    scale = W ** -0.5
    stores = []

    def grad(which):
        lhs, k, hbm = ((xg.at[0], 1, gg_hbm), (xg.at[0], 2, gu_hbm), (hid.at[0], 0, gd_hbm))[which]

        def tile(n, _):
            ds = pl.ds(pl.multiple_of(n * 256, 256), 256)
            rhs = hid[k] if which < 2 else xg[1]
            grads[which, ds, :] = (tn(lhs[:, ds], rhs) * scale).astype(BF16)
            return _

        lax.fori_loop(0, 3, tile, 0)
        st = pltpu.make_async_copy(grads.at[which], hbm, gsem.at[which])
        st.start()
        stores.append(st)

    def end(_):
        wait(rsem.at[last + FIN], frcv)
        for k, ref in enumerate((out_ref, gt_ref)):
            v = jnp.stack([fin[k, e] for e in OWN]) + frcv[k]
            ref[...] = unfold(v).astype(BF16)

    steps = {f.__name__: f for f in (
        zl_send, ag1, ag2x, ag2c, ready, mmx, mmc, rs1, rs2, el, fw, fp, fw2, outa, outb,
        o2a, o2b, o3a, o3b, fin_send, sent, grad, end)}
    for name, i in plan:
        steps[name](i)
    for st in stores:
        st.wait()


def move(*refs):
    srcs, dsts, bufs, isem, osem = refs[:5], refs[5:10], refs[10:15], refs[15], refs[16]
    parts = []
    for j in (2, 3, 4):
        for q in range(4):
            ds = pl.ds(q * W // 4, W // 4)
            parts.append((srcs[j].at[ds], bufs[j].at[ds], dsts[j].at[ds]))
    for j in (0, 1):
        parts.append((srcs[j], bufs[j], dsts[j]))
    loads = [pltpu.make_async_copy(s, b, isem.at[n]) for n, (s, b, _) in enumerate(parts)]
    stores = [pltpu.make_async_copy(b, d, osem.at[n]) for n, (_, b, d) in enumerate(parts)]
    for ld in loads:
        ld.start()
    for ld, st in zip(loads, stores):
        ld.wait()
        st.start()
    for st in stores:
        st.wait()


def local(tokens, cotangent, gate_weight, up_weight, down_weight):
    vmem = pl.BlockSpec(memory_space=pltpu.VMEM)
    hbm = pl.BlockSpec(memory_space=pl.ANY)
    small = jax.ShapeDtypeStruct((LOCAL, W), BF16)
    big = jax.ShapeDtypeStruct((W, W), BF16)
    results = pl.pallas_call(
        functools.partial(kernel, PLAN),
        name="swiglu",
        out_shape=(small, small, big, big, big),
        in_specs=[vmem, vmem, hbm, hbm, hbm],
        out_specs=(vmem, vmem, hbm, hbm, hbm),
        scratch_shapes=[
            pltpu.VMEM((W, W), BF16),
            pltpu.VMEM((W, W), BF16),
            pltpu.VMEM((W, W), BF16),
            pltpu.VMEM((2, 6, 4, 4, 16, HALF), BF16),
            pltpu.VMEM((2, W, W), BF16),
            pltpu.VMEM((3, W, HALF), F32),
            pltpu.VMEM((3, W, HALF), F32),
            pltpu.VMEM((3, W, HALF), F32),
            pltpu.VMEM((3, 3, W // 4, HALF), BF16),
            pltpu.VMEM((3, 3, W // 4, HALF), BF16),
            pltpu.VMEM((3, W, W), BF16),
            pltpu.VMEM((2, 6, 4, 4, 16, HALF), F32),
            pltpu.VMEM((2, 6, 4, 4, 16, HALF), BF16),
            pltpu.VMEM((2, 3, 6, 4, 16, HALF), BF16),
            pltpu.VMEM((max(SIZES), 4, 16, HALF), F32),
            pltpu.VMEM((2, 6, 4, 16, HALF), BF16),
            pltpu.VMEM((2, 6, 16, HALF), F32),
            pltpu.VMEM((2, 3, 6, 16, HALF), BF16),
            pltpu.VMEM((2, 6, 16, HALF), F32),
            pltpu.VMEM((2, 3, 16, HALF), F32),
            pltpu.VMEM((3, W, W), BF16),
            pltpu.SemaphoreType.DMA((SENDS,)),
            pltpu.SemaphoreType.DMA((RECVS,)),
            pltpu.SemaphoreType.DMA((3,)),
            pltpu.SemaphoreType.DMA((3,)),
        ],
        compiler_params=pltpu.CompilerParams(
            collective_id=0, has_side_effects=True, vmem_limit_bytes=56 << 20),
        cost_estimate=pl.CostEstimate(
            flops=18 * W ** 3, bytes_accessed=12 * W * W, transcendentals=W * W // 8),
    )(tokens, cotangent, gate_weight, up_weight, down_weight)
    return pl.pallas_call(
        move,
        name="move",
        out_shape=(small, small, big, big, big),
        in_specs=[hbm] * 5,
        out_specs=(hbm,) * 5,
        scratch_shapes=[pltpu.VMEM((LOCAL, W), BF16)] * 2 + [pltpu.VMEM((W, W), BF16)] * 3
        + [pltpu.SemaphoreType.DMA((14,))] * 2,
        compiler_params=pltpu.CompilerParams(vmem_limit_bytes=60 << 20),
    )(*results)


def solution(mesh):
    by_token = P(("depth", "col"), "row")
    by_model = P("row", ("depth", "col"))
    return jax.shard_map(
        local,
        mesh=mesh,
        in_specs=(by_token, by_token, by_model, by_model, by_token),
        out_specs=(by_token, by_token, by_model, by_model, by_token),
        check_vma=False,
    )
```

```python
import functools

import jax
import jax.numpy as jnp
from jax import lax
from jax.experimental import pallas as pl
from jax.experimental.pallas import tpu as pltpu
from jax.sharding import PartitionSpec as P

F32 = jnp.float32
BF16 = jnp.bfloat16
W = 768
HALF = W // 2
LOCAL = 24
UNIT = 128

SIZES = (1, 1, 1, 1, 1, 1)
OWN = (0, 1, 5)
OTHER = (2, 3, 4)

X1, C1, X2, C2, CORE, ZA, ZB, ZC, GN, GP, GF, GC, O1, G1, O2, G2 = range(16)
KINDS = 16
ZL, FIN = 0, 3
SENDS = KINDS + 2
RECVS = KINDS * len(SIZES) + 4

DIRECT = (5,)

PLAN = (
    ("ag1", 1), ("ready", 0), ("ag1", 0), ("ag2x", 1), ("zl_send", 1), ("ag2c", 1),
    ("ag1", 3), ("zl_send", 2), ("ag2x", 0), ("ag2c", 0), ("zl_send", 0), ("mmx", 1),
    ("mmc", 1), ("ag2c", 3), ("ag1", 2), ("rs1", 1), ("ag2x", 3), ("mmc", 0),
    ("mmx", 0), ("ag2c", 2), ("rs1", 0), ("ag1", 4), ("ag1", 5), ("mmc", 3),
    ("ag2x", 2), ("mmx", 3), ("rs2", 1), ("rs1", 3), ("mmx", 2), ("rs2", 0),
    ("mmc", 2), ("rs1", 2), ("rs2", 3), ("el", 1), ("el", 0), ("ag2x", 5),
    ("ag2c", 5), ("ag2x", 4), ("ag2c", 4), ("rs2", 2), ("fw", 1), ("mmc", 5),
    ("el", 3), ("fp", 1), ("mmc", 4), ("mmx", 4), ("rs1", 4), ("fw2", 1),
    ("fp", 0), ("fw", 0), ("mmx", 5), ("fp", 3), ("outa", 1), ("el", 2),
    ("outb", 1), ("o2a", 1), ("rs2", 4), ("fw", 3), ("fw", 2), ("fw2", 0),
    ("rs1", 5), ("outa", 0), ("el", 4), ("fp", 2), ("outb", 0), ("o2a", 0),
    ("fw2", 3), ("outa", 3), ("fw2", 2), ("rs2", 5), ("outb", 3), ("outa", 2),
    ("fw", 4), ("grad0", 0), ("el", 5), ("fp", 4), ("o2b", 3), ("outb", 2),
    ("grad1", 0), ("fw2", 4), ("o2b", 0), ("o2b", 1), ("o3a", 0), ("outa", 4),
    ("outb", 4), ("grad2", 0), ("o3b", 0), ("o2b", 2), ("fp", 5), ("o2a", 2),
    ("o3a", 1), ("fw", 5), ("o2a", 3), ("o3b", 3), ("fw2", 5), ("o2b", 4),
    ("o3b", 2), ("o2a", 4), ("outa", 5), ("outb", 5), ("o3a", 2), ("grad0", 1),
    ("o3a", 4), ("o3b", 1), ("o3a", 3), ("o3b", 4), ("fin_send", 0), ("o2a", 5),
    ("o2b", 5), ("grad2", 1), ("grad1", 1), ("o3a", 5), ("o3b", 5), ("sent", 0),
    ("end", 0),
)


def nt(a, b):
    return lax.dot_general(a, b, (((1,), (1,)), ((), ())), preferred_element_type=F32)


def nn(a, b):
    return jnp.dot(a, b, preferred_element_type=F32)


def tn(a, b):
    return lax.dot_general(a, b, (((0,), (0,)), ((), ())), preferred_element_type=F32)


def fold(v):
    v = v.reshape(v.shape[0] // 8, 8, W)
    return jnp.concatenate([v[:, :, :HALF], v[:, :, HALF:]], axis=1)


def unfold(v):
    v = jnp.concatenate([v[:, :8], v[:, 8:]], axis=2)
    return v.reshape(v.shape[0] * 8, W)


def kernel(plan, x_hbm, c_hbm, wg_hbm, wu_hbm, wd_hbm,
           out_ref, gt_ref, gg, gu, gd,
           x_in, c_in, acc, wg, wu, wd, xc, xg, csnd, crcv, part, zsnd, zrcv, hid,
           pf, psnd, p1rcv, sf, s1snd, s1own, p2rcv, fin, frcv,
           ssem, rsem, lsem):
    depth, row, xx = lax.axis_index("depth"), lax.axis_index("row"), lax.axis_index("col")
    zl, y, zh, a = depth // 4, depth % 4, row // 2, row % 2
    nxt, prv, opp = (zh + 1 + 2 * a) % 4, (zh + 3 + 2 * a) % 4, (zh + 2) % 4

    def dev(zl_=zl, y_=y, zh_=zh, a_=a, x_=xx):
        return (zl_ * 4 + y_, zh_ * 2 + a_, x_)

    others = ([dev(zl_=1 - zl), dev(a_=1 - a), dev(zh_=nxt), dev(zh_=prv), dev(zh_=opp)]
              + [dev(x_=(xx + j) % 4) for j in (1, 2, 3)]
              + [dev(y_=(y + j) % 4) for j in (1, 2, 3)])
    mine = pl.ds(pl.multiple_of(a * HALF, 128), HALF)
    theirs = pl.ds(pl.multiple_of((1 - a) * HALF, 128), HALF)
    def units(i):
        return slice(sum(SIZES[:i]), sum(SIZES[:i + 1]))

    def rows(i):
        return slice(UNIT * sum(SIZES[:i]), UNIT * sum(SIZES[:i + 1]))

    def quarter(i):
        return slice(UNIT // 4 * sum(SIZES[:i]), UNIT // 4 * sum(SIZES[:i + 1]))

    def piece(i, q):
        n = UNIT // 4 * SIZES[i]
        return pl.ds(pl.multiple_of(UNIT * sum(SIZES[:i]) + n * q, 32), n)

    def push(ssem_at, rsem_at, src, dst, to):
        pltpu.make_async_remote_copy(
            src_ref=src, dst_ref=dst, send_sem=ssem.at[ssem_at], recv_sem=rsem.at[rsem_at],
            device_id=to, device_id_type=pl.DeviceIdType.MESH).start()

    def send(i, k, src, dst, to):
        push(k, KINDS * i + k, src, dst, to)

    def wait(sem, ref):
        pltpu.make_async_copy(ref, ref, sem).wait()

    def got(i, k, ref):
        wait(rsem.at[KINDS * i + k], ref)

    last = KINDS * len(SIZES)

    barrier = pltpu.get_barrier_semaphore()
    for o in others:
        pl.semaphore_signal(barrier, inc=1, device_id=o, device_id_type=pl.DeviceIdType.MESH)
    loads = [pltpu.make_async_copy(s, d, lsem.at[j])
             for j, (s, d) in enumerate(((x_hbm, x_in), (c_hbm, c_in), (wg_hbm, wg),
                                         (wu_hbm, wu), (wd_hbm, wd)))]
    for ld in loads:
        ld.start()
    for k, ref in enumerate((x_in, c_in)):
        loads[k].wait()
        v = fold(ref[...].astype(F32)).astype(BF16)
        for u in range(3):
            xc[k, OWN[u], y, xx] = v[u]
    pl.semaphore_wait(barrier, len(others))

    def zl_send(u):
        push(KINDS, last + ZL + u,
             xc.at[:, OWN[u], y, xx], xc.at[:, OTHER[u], y, xx], dev(zl_=1 - zl))

    def ag1(i):
        es = units(i)
        for e in range(es.start, es.stop):
            if e in OTHER:
                wait(rsem.at[last + ZL + OTHER.index(e)], xc.at[:, e, y, xx])
        for j in (1, 2, 3):
            blk = xc.at[0, es, y, xx]
            send(i, X1, blk, blk, dev(x_=(xx + j) % 4))
            blk = xc.at[1, es, y, xx]
            send(i, C1, blk, blk, dev(y_=(y + j) % 4))

    def ag2x(i):
        es = units(i)
        got(i, X1, xc.at[0, es, y, :3])
        for j in (1, 2, 3):
            blk = xc.at[0, es, y]
            send(i, X2, blk, blk, dev(y_=(y + j) % 4))

    def ag2c(i):
        es = units(i)
        got(i, C1, xc.at[1, es, :3, xx])
        for j in (1, 2, 3):
            blk = xc.at[1, es, :, xx]
            send(i, C2, blk, blk, dev(x_=(xx + j) % 4))

    def ready(_):
        for ld in loads[2:]:
            ld.wait()

    def gathered(i, k):
        v = xc[k, units(i)].reshape(16 * SIZES[i], 16, HALF)
        v = unfold(v.astype(F32)).astype(BF16)
        xg[k, rows(i)] = v
        return v

    def mmx(i):
        rs = rows(i)
        got(i, X2, xc.at[0, units(i), :3])
        xs = gathered(i, 0)
        for j, w in ((0, wg), (1, wu)):
            csnd[j, rs] = nn(xs, w[:, theirs])
            send(i, CORE, csnd.at[j, rs], crcv.at[j, rs], dev(a_=1 - a))
        part[0, rs] = nn(xs, wg[:, mine])
        part[1, rs] = nn(xs, wu[:, mine])

    def mmc(i):
        rs = rows(i)
        got(i, C2, xc.at[1, units(i), :3])
        cs = gathered(i, 1)
        csnd[2, rs] = nt(cs, wd[theirs, :])
        send(i, CORE, csnd.at[2, rs], crcv.at[2, rs], dev(a_=1 - a))
        part[2, rs] = nt(cs, wd[mine, :])

    def rs1(i):
        rs, qs = rows(i), quarter(i)
        got(i, CORE, crcv.at[:, rs])
        part[:, rs] = part[:, rs] + crcv[:, rs]
        zsnd[0, :, qs] = part[:, piece(i, opp)].astype(BF16)
        send(i, ZA, zsnd.at[0, :, qs], zrcv.at[0, :, qs], dev(zh_=nxt))
        zsnd[1, :, qs] = part[:, piece(i, prv)].astype(BF16)
        send(i, ZB, zsnd.at[1, :, qs], zrcv.at[1, :, qs], dev(zh_=prv))

    def rs2(i):
        qs = quarter(i)
        got(i, ZA, zrcv.at[0, :, qs])
        zsnd[2, :, qs] = (part[:, piece(i, nxt)] + zrcv[0, :, qs].astype(F32)).astype(BF16)
        send(i, ZC, zsnd.at[2, :, qs], zrcv.at[2, :, qs], dev(zh_=nxt))

    def el(i):
        qs, ps = quarter(i), piece(i, zh)
        got(i, ZB, zrcv.at[1, :, qs])
        got(i, ZC, zrcv.at[2, :, qs])
        tot = part[:, ps] + zrcv[1, :, qs].astype(F32) + zrcv[2, :, qs].astype(F32)
        gate, up, slope = tot[0], tot[1], tot[2]
        sig = 1.0 / (1.0 + jnp.exp(-gate))
        act = gate * sig
        hid[0, ps, mine] = (act * up).astype(BF16)
        hid[1, ps, mine] = (slope * up * sig * (1.0 + gate * (1.0 - sig))).astype(BF16)
        hid[2, ps, mine] = (slope * act).astype(BF16)
        blk = hid.at[:, ps, mine]
        send(i, GN, blk, blk, dev(zh_=nxt))
        send(i, GP, blk, blk, dev(zh_=prv))
        if i in DIRECT:
            send(i, GF, blk, blk, dev(zh_=opp))
        send(i, GC, blk, blk, dev(a_=1 - a))

    def fw(i):
        blk = hid.at[:, piece(i, prv), mine]
        got(i, GN, blk)
        if i not in DIRECT:
            send(i, GF, blk, blk, dev(zh_=nxt))
        send(i, GC, blk, blk, dev(a_=1 - a))

    def fp(i):
        blk = hid.at[:, piece(i, nxt), mine]
        got(i, GP, blk)
        send(i, GC, blk, blk, dev(a_=1 - a))

    def fw2(i):
        blk = hid.at[:, piece(i, opp), mine]
        got(i, GF, blk)
        send(i, GC, blk, blk, dev(a_=1 - a))

    def outa(i):
        rs, es, n = rows(i), units(i), SIZES[i]
        got(i, GC, hid.at[:, rs, theirs])
        p = fold(nn(hid[0, rs], wd[...])).reshape(n, 4, 4, 16, HALF)
        pf[0, es] = p
        psnd[0, es] = p.astype(BF16)
        for j in (1, 2, 3):
            to = (xx + j) % 4
            send(i, O1, psnd.at[0, es, :, to], p1rcv.at[0, j - 1, es], dev(x_=to))

    def outb(i):
        rs, es, n = rows(i), units(i), SIZES[i]
        p = fold(nt(hid[1, rs], wg[...]) + nt(hid[2, rs], wu[...])).reshape(n, 4, 4, 16, HALF)
        pf[1, es] = p
        psnd[1, es] = p.astype(BF16)
        for j in (1, 2, 3):
            to = (y + j) % 4
            send(i, G1, psnd.at[1, es, to], p1rcv.at[1, j - 1, es], dev(y_=to))

    def second(i, k, t):
        es = units(i)
        for j in range(3):
            t = t + p1rcv[k, j, es].astype(F32)
        sf[:SIZES[i]] = t
        s1snd[k, es] = t.astype(BF16)

    def o2a(i):
        es = units(i)
        got(i, O1, p1rcv.at[0, :, es])
        second(i, 0, pf[0, es, :, xx])
        for j in (1, 2, 3):
            to = (y + j) % 4
            send(i, O2, s1snd.at[0, es, to], p2rcv.at[0, j - 1, es], dev(y_=to))
        s1own[0, es] = sf[:SIZES[i], y]

    def o2b(i):
        es = units(i)
        got(i, G1, p1rcv.at[1, :, es])
        second(i, 1, pf[1, es, y])
        for j in (1, 2, 3):
            to = (xx + j) % 4
            send(i, G2, s1snd.at[1, es, to], p2rcv.at[1, j - 1, es], dev(x_=to))
        s1own[1, es] = sf[:SIZES[i], xx]

    def third(i, k, kind):
        es = units(i)
        got(i, kind, p2rcv.at[k, :, es])
        t = s1own[k, es]
        for j in range(3):
            t = t + p2rcv[k, j, es].astype(F32)
        fin[k, es] = t

    def o3a(i):
        third(i, 0, O2)

    def o3b(i):
        third(i, 1, G2)

    def fin_send(_):
        push(KINDS + 1, last + FIN, fin.at[:, OTHER[0]:OTHER[-1] + 1], frcv, dev(zl_=1 - zl))

    def sent(_):
        block, half = xc.at[0, :, 0, :3], hid.at[:, :, :HALF]
        for k, ref in ((X1, block), (C1, block), (X2, xc.at[0, :, :3]), (C2, xc.at[1, :, :3]),
                       (CORE, csnd), (ZA, zsnd.at[0]), (ZB, zsnd.at[1]), (ZC, zsnd.at[2]),
                       (GN, zsnd.at[0]), (GP, zsnd.at[1]), (GF, zsnd.at[2]), (GC, half),
                       (O1, p1rcv.at[0]), (G1, p1rcv.at[1]), (O2, p2rcv.at[0]),
                       (G2, p2rcv.at[1]), (KINDS, xc.at[:, :3, 0, 0]), (KINDS + 1, frcv)):
            wait(ssem.at[k], ref)

    scale = W ** -0.5

    def grads(i, which):
        rs = slice(512 * i, 512 + 256 * i)
        lhs, rhs, res = ((xg.at[0, rs], hid[1, rs], gg), (xg.at[0, rs], hid[2, rs], gu),
                         (hid.at[0, rs], xg[1, rs], gd))[which]

        def tile(n, _):
            ds = pl.ds(pl.multiple_of(n * 256, 256), 256)
            t = tn(lhs[:, ds], rhs)
            if i == 0:
                acc[which, ds, :] = t
            else:
                res[ds, :] = ((t + acc[which, ds, :]) * scale).astype(BF16)
            return _

        lax.fori_loop(0, 3, tile, 0)

    def grad0(i):
        grads(i, 0)

    def grad1(i):
        grads(i, 1)

    def grad2(i):
        grads(i, 2)

    def end(_):
        wait(rsem.at[last + FIN], frcv)
        for k, ref in enumerate((out_ref, gt_ref)):
            v = jnp.stack([fin[k, e] for e in OWN]) + frcv[k]
            ref[...] = unfold(v).astype(BF16)

    steps = {f.__name__: f for f in (
        zl_send, ag1, ag2x, ag2c, ready, mmx, mmc, rs1, rs2, el, fw, fp, fw2, outa, outb,
        o2a, o2b, o3a, o3b, fin_send, sent, grad0, grad1, grad2, end)}
    for name, i in plan:
        steps[name](i)


def move(*refs):
    stores = [pltpu.make_async_copy(s, d, refs[10].at[n])
              for n, (s, d) in enumerate(zip(refs[:5], refs[5:10]))]
    for st in stores:
        st.start()
    for st in stores:
        st.wait()


def local(tokens, cotangent, gate_weight, up_weight, down_weight):
    vmem = pl.BlockSpec(memory_space=pltpu.VMEM)
    hbm = pl.BlockSpec(memory_space=pl.ANY)
    small = jax.ShapeDtypeStruct((LOCAL, W), BF16)
    big = jax.ShapeDtypeStruct((W, W), BF16)
    results = pl.pallas_call(
        functools.partial(kernel, PLAN),
        name="swiglu",
        out_shape=[pltpu.VMEM(t.shape, t.dtype) for t in (small, small, big, big, big)],
        in_specs=[hbm] * 5,
        out_specs=[vmem] * 5,
        scratch_shapes=[
            pltpu.VMEM((LOCAL, W), BF16),
            pltpu.VMEM((LOCAL, W), BF16),
            pltpu.VMEM((3, W, W), F32),
            pltpu.VMEM((W, W), BF16),
            pltpu.VMEM((W, W), BF16),
            pltpu.VMEM((W, W), BF16),
            pltpu.VMEM((2, 6, 4, 4, 16, HALF), BF16),
            pltpu.VMEM((2, W, W), BF16),
            pltpu.VMEM((3, W, HALF), F32),
            pltpu.VMEM((3, W, HALF), F32),
            pltpu.VMEM((3, W, HALF), F32),
            pltpu.VMEM((3, 3, W // 4, HALF), BF16),
            pltpu.VMEM((3, 3, W // 4, HALF), BF16),
            pltpu.VMEM((3, W, W), BF16),
            pltpu.VMEM((2, 6, 4, 4, 16, HALF), F32),
            pltpu.VMEM((2, 6, 4, 4, 16, HALF), BF16),
            pltpu.VMEM((2, 3, 6, 4, 16, HALF), BF16),
            pltpu.VMEM((max(SIZES), 4, 16, HALF), F32),
            pltpu.VMEM((2, 6, 4, 16, HALF), BF16),
            pltpu.VMEM((2, 6, 16, HALF), F32),
            pltpu.VMEM((2, 3, 6, 16, HALF), BF16),
            pltpu.VMEM((2, 6, 16, HALF), F32),
            pltpu.VMEM((2, 3, 16, HALF), F32),
            pltpu.SemaphoreType.DMA((SENDS,)),
            pltpu.SemaphoreType.DMA((RECVS,)),
            pltpu.SemaphoreType.DMA((5,)),
        ],
        compiler_params=pltpu.CompilerParams(
            collective_id=0, has_side_effects=True, vmem_limit_bytes=56 << 20),
        cost_estimate=pl.CostEstimate(
            flops=18 * W ** 3, bytes_accessed=12 * W * W, transcendentals=W * W // 8),
    )(tokens, cotangent, gate_weight, up_weight, down_weight)
    return pl.pallas_call(
        move,
        name="move",
        out_shape=(small, small, big, big, big),
        in_specs=[vmem] * 5,
        out_specs=(hbm,) * 5,
        scratch_shapes=[pltpu.SemaphoreType.DMA((5,))],
    )(*results)


def solution(mesh):
    by_token = P(("depth", "col"), "row")
    by_model = P("row", ("depth", "col"))
    return jax.shard_map(
        local,
        mesh=mesh,
        in_specs=(by_token, by_token, by_model, by_model, by_token),
        out_specs=(by_token, by_token, by_model, by_model, by_token),
        check_vma=False,
    )
```

```python
import functools

import jax
import jax.numpy as jnp
from jax import lax
from jax.experimental import pallas as pl
from jax.experimental.pallas import tpu as pltpu
from jax.sharding import PartitionSpec as P

F32 = jnp.float32
BF16 = jnp.bfloat16
W = 768
HALF = W // 2
LOCAL = 24
UNIT = 128

SIZES = (1, 1, 1, 1, 1, 1)
OWN = (0, 4, 5)
OTHER = (1, 2, 3)

X1, C1, X2, C2, CORE, ZA, ZB, ZC, GN, GP, GF, GC, O1, G1, O2, G2 = range(16)
KINDS = 16
ZL, FIN = 0, 3
SENDS = KINDS + 2
RECVS = KINDS * len(SIZES) + 4

DIRECT = ()

PLAN = (
    ("zl_send", 0), ("ag1", 5), ("zl_send", 1), ("zl_send", 2), ("ag1", 4), ("ag1", 0),
    ("ready", 0), ("ag1", 1), ("ag2c", 5), ("ag2x", 5), ("ag2x", 1), ("ag2c", 1),
    ("mmc", 5), ("mmx", 5), ("ag1", 2), ("ag2x", 4), ("ag2c", 4), ("mmx", 1),
    ("rs1", 5), ("mmc", 1), ("ag1", 3), ("ag2c", 0), ("ag2x", 2), ("rs1", 1),
    ("mmx", 4), ("ag2x", 3), ("mmc", 4), ("rs2", 5), ("ag2c", 2), ("mmc", 0),
    ("rs1", 4), ("rs2", 1), ("mmx", 3), ("mmx", 2), ("mmc", 2), ("el", 5),
    ("ag2x", 0), ("ag2c", 3), ("rs1", 2), ("el", 1), ("mmc", 3), ("rs1", 3),
    ("fw", 5), ("rs2", 2), ("fw", 1), ("mmx", 0), ("rs2", 3), ("rs1", 0),
    ("fw2", 5), ("el", 2), ("fp", 5), ("fw2", 1), ("fp", 1), ("outa", 1),
    ("el", 3), ("outb", 1), ("outa", 5), ("rs2", 4), ("fw", 2), ("fp", 2),
    ("outb", 5), ("rs2", 0), ("fw", 3), ("o2b", 1), ("fp", 3), ("o2a", 1),
    ("o2a", 5), ("el", 4), ("o3a", 1), ("fw2", 2), ("el", 0), ("outa", 2),
    ("fw2", 3), ("o2b", 5), ("outb", 2), ("outa", 3), ("fw", 4), ("fp", 4),
    ("outb", 3), ("o3b", 1), ("fw", 0), ("o2a", 2), ("fw2", 4), ("o2b", 2),
    ("fp", 0), ("o2a", 3), ("o3a", 5), ("o2b", 3), ("fw2", 0), ("outa", 4),
    ("outb", 4), ("outa", 0), ("grad2", 0), ("outb", 0), ("o3a", 2), ("o3a", 3),
    ("o3b", 2), ("o3b", 3), ("fin_send", 0), ("grad1", 0), ("grad2", 1), ("o2a", 4),
    ("o2b", 4), ("grad1", 1), ("o2a", 0), ("o3b", 5), ("o2b", 0), ("grad0", 0),
    ("o3a", 4), ("grad0", 1), ("o3a", 0), ("o3b", 0), ("o3b", 4), ("sent", 0),
    ("end", 0),
)


def nt(a, b):
    return lax.dot_general(a, b, (((1,), (1,)), ((), ())), preferred_element_type=F32)


def nn(a, b):
    return jnp.dot(a, b, preferred_element_type=F32)


def tn(a, b):
    return lax.dot_general(a, b, (((0,), (0,)), ((), ())), preferred_element_type=F32)


def fold(v):
    v = v.reshape(v.shape[0] // 8, 8, W)
    return jnp.concatenate([v[:, :, :HALF], v[:, :, HALF:]], axis=1)


def unfold(v):
    v = jnp.concatenate([v[:, :8], v[:, 8:]], axis=2)
    return v.reshape(v.shape[0] * 8, W)


def kernel(plan, x_hbm, c_hbm, wg_hbm, wu_hbm, wd_hbm,
           out_ref, gt_ref, gg_hbm, gu_hbm, gd_hbm,
           x_in, c_in, acc, grad, wg, wu, wd, xc, xg, csnd, crcv, part, zsnd, zrcv, hid,
           pf, psnd, p1rcv, sf, s1snd, s1own, p2rcv, fin, frcv,
           ssem, rsem, lsem, gsem):
    depth, row, xx = lax.axis_index("depth"), lax.axis_index("row"), lax.axis_index("col")
    zl, y, zh, a = depth // 4, depth % 4, row // 2, row % 2
    nxt, prv, opp = (zh + 1 + 2 * a) % 4, (zh + 3 + 2 * a) % 4, (zh + 2) % 4

    def dev(zl_=zl, y_=y, zh_=zh, a_=a, x_=xx):
        return (zl_ * 4 + y_, zh_ * 2 + a_, x_)

    others = ([dev(zl_=1 - zl), dev(a_=1 - a), dev(zh_=nxt), dev(zh_=prv), dev(zh_=opp)]
              + [dev(x_=(xx + j) % 4) for j in (1, 2, 3)]
              + [dev(y_=(y + j) % 4) for j in (1, 2, 3)])
    mine = pl.ds(pl.multiple_of(a * HALF, 128), HALF)
    theirs = pl.ds(pl.multiple_of((1 - a) * HALF, 128), HALF)
    def units(i):
        return slice(sum(SIZES[:i]), sum(SIZES[:i + 1]))

    def rows(i):
        return slice(UNIT * sum(SIZES[:i]), UNIT * sum(SIZES[:i + 1]))

    def quarter(i):
        return slice(UNIT // 4 * sum(SIZES[:i]), UNIT // 4 * sum(SIZES[:i + 1]))

    def piece(i, q):
        n = UNIT // 4 * SIZES[i]
        return pl.ds(pl.multiple_of(UNIT * sum(SIZES[:i]) + n * q, 32), n)

    def push(ssem_at, rsem_at, src, dst, to):
        pltpu.make_async_remote_copy(
            src_ref=src, dst_ref=dst, send_sem=ssem.at[ssem_at], recv_sem=rsem.at[rsem_at],
            device_id=to, device_id_type=pl.DeviceIdType.MESH).start()

    def send(i, k, src, dst, to):
        push(k, KINDS * i + k, src, dst, to)

    def wait(sem, ref):
        pltpu.make_async_copy(ref, ref, sem).wait()

    def got(i, k, ref):
        wait(rsem.at[KINDS * i + k], ref)

    last = KINDS * len(SIZES)

    barrier = pltpu.get_barrier_semaphore()
    for o in others:
        pl.semaphore_signal(barrier, inc=1, device_id=o, device_id_type=pl.DeviceIdType.MESH)
    loads = [pltpu.make_async_copy(s, d, lsem.at[j])
             for j, (s, d) in enumerate(((x_hbm, x_in), (c_hbm, c_in), (wg_hbm, wg),
                                         (wu_hbm, wu), (wd_hbm, wd)))]
    for ld in loads:
        ld.start()
    for k, ref in enumerate((x_in, c_in)):
        loads[k].wait()
        v = fold(ref[...].astype(F32)).astype(BF16)
        for u in range(3):
            xc[k, OWN[u], y, xx] = v[u]
    pl.semaphore_wait(barrier, len(others))

    def zl_send(u):
        push(KINDS, last + ZL + u,
             xc.at[:, OWN[u], y, xx], xc.at[:, OTHER[u], y, xx], dev(zl_=1 - zl))

    def ag1(i):
        es = units(i)
        for e in range(es.start, es.stop):
            if e in OTHER:
                wait(rsem.at[last + ZL + OTHER.index(e)], xc.at[:, e, y, xx])
        for j in (1, 2, 3):
            blk = xc.at[0, es, y, xx]
            send(i, X1, blk, blk, dev(x_=(xx + j) % 4))
            blk = xc.at[1, es, y, xx]
            send(i, C1, blk, blk, dev(y_=(y + j) % 4))

    def ag2x(i):
        es = units(i)
        got(i, X1, xc.at[0, es, y, :3])
        for j in (1, 2, 3):
            blk = xc.at[0, es, y]
            send(i, X2, blk, blk, dev(y_=(y + j) % 4))

    def ag2c(i):
        es = units(i)
        got(i, C1, xc.at[1, es, :3, xx])
        for j in (1, 2, 3):
            blk = xc.at[1, es, :, xx]
            send(i, C2, blk, blk, dev(x_=(xx + j) % 4))

    def ready(_):
        for ld in loads[2:]:
            ld.wait()

    def gathered(i, k):
        v = xc[k, units(i)].reshape(16 * SIZES[i], 16, HALF)
        v = unfold(v.astype(F32)).astype(BF16)
        xg[k, rows(i)] = v
        return v

    def mmx(i):
        rs = rows(i)
        got(i, X2, xc.at[0, units(i), :3])
        xs = gathered(i, 0)
        for j, w in ((0, wg), (1, wu)):
            csnd[j, rs] = nn(xs, w[:, theirs])
            send(i, CORE, csnd.at[j, rs], crcv.at[j, rs], dev(a_=1 - a))
        part[0, rs] = nn(xs, wg[:, mine])
        part[1, rs] = nn(xs, wu[:, mine])

    def mmc(i):
        rs = rows(i)
        got(i, C2, xc.at[1, units(i), :3])
        cs = gathered(i, 1)
        csnd[2, rs] = nt(cs, wd[theirs, :])
        send(i, CORE, csnd.at[2, rs], crcv.at[2, rs], dev(a_=1 - a))
        part[2, rs] = nt(cs, wd[mine, :])

    def rs1(i):
        rs, qs = rows(i), quarter(i)
        got(i, CORE, crcv.at[:, rs])
        part[:, rs] = part[:, rs] + crcv[:, rs]
        zsnd[0, :, qs] = part[:, piece(i, opp)].astype(BF16)
        send(i, ZA, zsnd.at[0, :, qs], zrcv.at[0, :, qs], dev(zh_=nxt))
        zsnd[1, :, qs] = part[:, piece(i, prv)].astype(BF16)
        send(i, ZB, zsnd.at[1, :, qs], zrcv.at[1, :, qs], dev(zh_=prv))

    def rs2(i):
        qs = quarter(i)
        got(i, ZA, zrcv.at[0, :, qs])
        zsnd[2, :, qs] = (part[:, piece(i, nxt)] + zrcv[0, :, qs].astype(F32)).astype(BF16)
        send(i, ZC, zsnd.at[2, :, qs], zrcv.at[2, :, qs], dev(zh_=nxt))

    def el(i):
        qs, ps = quarter(i), piece(i, zh)
        got(i, ZB, zrcv.at[1, :, qs])
        got(i, ZC, zrcv.at[2, :, qs])
        tot = part[:, ps] + zrcv[1, :, qs].astype(F32) + zrcv[2, :, qs].astype(F32)
        gate, up, slope = tot[0], tot[1], tot[2]
        sig = 1.0 / (1.0 + jnp.exp(-gate))
        act = gate * sig
        hid[0, ps, mine] = (act * up).astype(BF16)
        hid[1, ps, mine] = (slope * up * sig * (1.0 + gate * (1.0 - sig))).astype(BF16)
        hid[2, ps, mine] = (slope * act).astype(BF16)
        blk = hid.at[:, ps, mine]
        send(i, GN, blk, blk, dev(zh_=nxt))
        send(i, GP, blk, blk, dev(zh_=prv))
        if i in DIRECT:
            send(i, GF, blk, blk, dev(zh_=opp))
        send(i, GC, blk, blk, dev(a_=1 - a))

    def fw(i):
        blk = hid.at[:, piece(i, prv), mine]
        got(i, GN, blk)
        if i not in DIRECT:
            send(i, GF, blk, blk, dev(zh_=nxt))
        send(i, GC, blk, blk, dev(a_=1 - a))

    def fp(i):
        blk = hid.at[:, piece(i, nxt), mine]
        got(i, GP, blk)
        send(i, GC, blk, blk, dev(a_=1 - a))

    def fw2(i):
        blk = hid.at[:, piece(i, opp), mine]
        got(i, GF, blk)
        send(i, GC, blk, blk, dev(a_=1 - a))

    def outa(i):
        rs, es, n = rows(i), units(i), SIZES[i]
        got(i, GC, hid.at[:, rs, theirs])
        p = fold(nn(hid[0, rs], wd[...])).reshape(n, 4, 4, 16, HALF)
        pf[0, es] = p
        psnd[0, es] = p.astype(BF16)
        for j in (1, 2, 3):
            to = (xx + j) % 4
            send(i, O1, psnd.at[0, es, :, to], p1rcv.at[0, j - 1, es], dev(x_=to))

    def outb(i):
        rs, es, n = rows(i), units(i), SIZES[i]
        p = fold(nt(hid[1, rs], wg[...]) + nt(hid[2, rs], wu[...])).reshape(n, 4, 4, 16, HALF)
        pf[1, es] = p
        psnd[1, es] = p.astype(BF16)
        for j in (1, 2, 3):
            to = (y + j) % 4
            send(i, G1, psnd.at[1, es, to], p1rcv.at[1, j - 1, es], dev(y_=to))

    def second(i, k, t):
        es = units(i)
        for j in range(3):
            t = t + p1rcv[k, j, es].astype(F32)
        sf[:SIZES[i]] = t
        s1snd[k, es] = t.astype(BF16)

    def o2a(i):
        es = units(i)
        got(i, O1, p1rcv.at[0, :, es])
        second(i, 0, pf[0, es, :, xx])
        for j in (1, 2, 3):
            to = (y + j) % 4
            send(i, O2, s1snd.at[0, es, to], p2rcv.at[0, j - 1, es], dev(y_=to))
        s1own[0, es] = sf[:SIZES[i], y]

    def o2b(i):
        es = units(i)
        got(i, G1, p1rcv.at[1, :, es])
        second(i, 1, pf[1, es, y])
        for j in (1, 2, 3):
            to = (xx + j) % 4
            send(i, G2, s1snd.at[1, es, to], p2rcv.at[1, j - 1, es], dev(x_=to))
        s1own[1, es] = sf[:SIZES[i], xx]

    def third(i, k, kind):
        es = units(i)
        got(i, kind, p2rcv.at[k, :, es])
        t = s1own[k, es]
        for j in range(3):
            t = t + p2rcv[k, j, es].astype(F32)
        fin[k, es] = t

    def o3a(i):
        third(i, 0, O2)

    def o3b(i):
        third(i, 1, G2)

    def fin_send(_):
        push(KINDS + 1, last + FIN, fin.at[:, OTHER[0]:OTHER[-1] + 1], frcv, dev(zl_=1 - zl))

    def sent(_):
        block, half = xc.at[0, :, 0, :3], hid.at[:, :, :HALF]
        for k, ref in ((X1, block), (C1, block), (X2, xc.at[0, :, :3]), (C2, xc.at[1, :, :3]),
                       (CORE, csnd), (ZA, zsnd.at[0]), (ZB, zsnd.at[1]), (ZC, zsnd.at[2]),
                       (GN, zsnd.at[0]), (GP, zsnd.at[1]), (GF, zsnd.at[2]), (GC, half),
                       (O1, p1rcv.at[0]), (G1, p1rcv.at[1]), (O2, p2rcv.at[0]),
                       (G2, p2rcv.at[1]), (KINDS, xc.at[:, :3, 0, 0]), (KINDS + 1, frcv)):
            wait(ssem.at[k], ref)

    scale = W ** -0.5
    stores = []

    def grads(i, which):
        rs = slice(512 * i, 512 + 256 * i)
        lhs, rhs, res = ((xg.at[0, rs], hid[1, rs], gg_hbm), (xg.at[0, rs], hid[2, rs], gu_hbm),
                         (hid.at[0, rs], xg[1, rs], gd_hbm))[which]

        def tile(n, _):
            ds = pl.ds(pl.multiple_of(n * 256, 256), 256)
            t = tn(lhs[:, ds], rhs)
            if i == 0:
                acc[which, ds, :] = t
            else:
                grad[which, ds, :] = ((t + acc[which, ds, :]) * scale).astype(BF16)
            return _

        lax.fori_loop(0, 3, tile, 0)
        if i == 1:
            st = pltpu.make_async_copy(grad.at[which], res, gsem.at[which])
            st.start()
            stores.append(st)

    def grad0(i):
        grads(i, 0)

    def grad1(i):
        grads(i, 1)

    def grad2(i):
        grads(i, 2)

    def end(_):
        wait(rsem.at[last + FIN], frcv)
        for k, ref in enumerate((out_ref, gt_ref)):
            v = jnp.stack([fin[k, e] for e in OWN]) + frcv[k]
            ref[...] = unfold(v).astype(BF16)

    steps = {f.__name__: f for f in (
        zl_send, ag1, ag2x, ag2c, ready, mmx, mmc, rs1, rs2, el, fw, fp, fw2, outa, outb,
        o2a, o2b, o3a, o3b, fin_send, sent, grad0, grad1, grad2, end)}
    for name, i in plan:
        steps[name](i)
    for st in stores:
        st.wait()


def move(*refs):
    srcs, dsts, bufs, isem, osem = refs[:5], refs[5:10], refs[10:15], refs[15], refs[16]
    parts = []
    for j in (2, 3, 4):
        for q in range(2):
            ds = pl.ds(q * HALF, HALF)
            parts.append((srcs[j].at[ds], bufs[j].at[ds], dsts[j].at[ds]))
    for j in (0, 1):
        parts.append((srcs[j], bufs[j], dsts[j]))
    loads = [pltpu.make_async_copy(s, b, isem.at[n]) for n, (s, b, _) in enumerate(parts)]
    stores = [pltpu.make_async_copy(b, d, osem.at[n]) for n, (_, b, d) in enumerate(parts)]
    for ld in loads:
        ld.start()
    for ld, st in zip(loads, stores):
        ld.wait()
        st.start()
    for st in stores:
        st.wait()


def local(tokens, cotangent, gate_weight, up_weight, down_weight):
    vmem = pl.BlockSpec(memory_space=pltpu.VMEM)
    hbm = pl.BlockSpec(memory_space=pl.ANY)
    small = jax.ShapeDtypeStruct((LOCAL, W), BF16)
    big = jax.ShapeDtypeStruct((W, W), BF16)
    results = pl.pallas_call(
        functools.partial(kernel, PLAN),
        name="swiglu",
        out_shape=(small, small, big, big, big),
        in_specs=[hbm] * 5,
        out_specs=(vmem, vmem, hbm, hbm, hbm),
        scratch_shapes=[
            pltpu.VMEM((LOCAL, W), BF16),
            pltpu.VMEM((LOCAL, W), BF16),
            pltpu.VMEM((3, W, W), F32),
            pltpu.VMEM((3, W, W), BF16),
            pltpu.VMEM((W, W), BF16),
            pltpu.VMEM((W, W), BF16),
            pltpu.VMEM((W, W), BF16),
            pltpu.VMEM((2, 6, 4, 4, 16, HALF), BF16),
            pltpu.VMEM((2, W, W), BF16),
            pltpu.VMEM((3, W, HALF), F32),
            pltpu.VMEM((3, W, HALF), F32),
            pltpu.VMEM((3, W, HALF), F32),
            pltpu.VMEM((3, 3, W // 4, HALF), BF16),
            pltpu.VMEM((3, 3, W // 4, HALF), BF16),
            pltpu.VMEM((3, W, W), BF16),
            pltpu.VMEM((2, 6, 4, 4, 16, HALF), F32),
            pltpu.VMEM((2, 6, 4, 4, 16, HALF), BF16),
            pltpu.VMEM((2, 3, 6, 4, 16, HALF), BF16),
            pltpu.VMEM((max(SIZES), 4, 16, HALF), F32),
            pltpu.VMEM((2, 6, 4, 16, HALF), BF16),
            pltpu.VMEM((2, 6, 16, HALF), F32),
            pltpu.VMEM((2, 3, 6, 16, HALF), BF16),
            pltpu.VMEM((2, 6, 16, HALF), F32),
            pltpu.VMEM((2, 3, 16, HALF), F32),
            pltpu.SemaphoreType.DMA((SENDS,)),
            pltpu.SemaphoreType.DMA((RECVS,)),
            pltpu.SemaphoreType.DMA((5,)),
            pltpu.SemaphoreType.DMA((3,)),
        ],
        compiler_params=pltpu.CompilerParams(
            collective_id=0, has_side_effects=True, vmem_limit_bytes=56 << 20),
        cost_estimate=pl.CostEstimate(
            flops=18 * W ** 3, bytes_accessed=12 * W * W, transcendentals=W * W // 8),
    )(tokens, cotangent, gate_weight, up_weight, down_weight)
    return pl.pallas_call(
        move,
        name="move",
        out_shape=(small, small, big, big, big),
        in_specs=[hbm] * 5,
        out_specs=(hbm,) * 5,
        scratch_shapes=[pltpu.VMEM((LOCAL, W), BF16)] * 2 + [pltpu.VMEM((W, W), BF16)] * 3
        + [pltpu.SemaphoreType.DMA((8,))] * 2,
        compiler_params=pltpu.CompilerParams(vmem_limit_bytes=60 << 20),
    )(*results)


def solution(mesh):
    by_token = P(("depth", "col"), "row")
    by_model = P("row", ("depth", "col"))
    return jax.shard_map(
        local,
        mesh=mesh,
        in_specs=(by_token, by_token, by_model, by_model, by_token),
        out_specs=(by_token, by_token, by_model, by_model, by_token),
        check_vma=False,
    )
```

```python
import functools

import jax
import jax.numpy as jnp
from jax import lax
from jax.experimental import pallas as pl
from jax.experimental.pallas import tpu as pltpu
from jax.sharding import PartitionSpec as P

F32 = jnp.float32
BF16 = jnp.bfloat16
W = 768
HALF = W // 2
LOCAL = 24
UNIT = 128

OWN = (0, 4, 5)
OTHER = (1, 2, 3)
WHOLE, NEAR, FAR = range(3)
CHUNKS = ((0, NEAR), (0, FAR), (1, WHOLE), (2, WHOLE), (3, WHOLE), (4, WHOLE), (5, WHOLE))

X1, C1, X2, C2, CORE, ZA, ZB, ZC, GN, GP, GF, GC, O1, G1, O2, G2 = range(16)
KINDS = 16
ZL, FIN = 0, 3
SENDS = KINDS + 2
RECVS = 14 * len(CHUNKS) + 2 * 6 + 4

DIRECT = ()

PLAN = (
    ("ag1", 0), ("zl_send", 2), ("ag1", 4), ("ag2x", 0), ("ag2c", 0), ("zl_send", 1),
    ("ready", 0), ("ag2x", 1), ("zl_send", 0), ("ag2c", 1), ("ag1", 3), ("ag2x", 5),
    ("ag2c", 5), ("mmx", 0), ("mmc", 0), ("ag2x", 4), ("rs1", 0), ("mmc", 1),
    ("mmx", 1), ("ag2c", 4), ("mmx", 5), ("rs1", 1), ("mmc", 5), ("ag1", 1),
    ("ag1", 5), ("rs2", 0), ("rs1", 5), ("mmx", 4), ("ag1", 2), ("mmc", 4),
    ("ag2x", 2), ("rs2", 1), ("ag2c", 2), ("el", 0), ("rs1", 4), ("el", 1),
    ("rs2", 5), ("mmx", 2), ("ag2x", 3), ("mmc", 2), ("ag2c", 3), ("fw", 0),
    ("rs1", 2), ("fw", 1), ("mmx", 3), ("rs2", 4), ("mmc", 3), ("el", 5),
    ("rs2", 2), ("ag2x", 6), ("ag2c", 6), ("rs1", 3), ("fp", 0), ("fw2", 0),
    ("outa", 0), ("el", 4), ("outb", 0), ("fw", 5), ("fw2", 1), ("fp", 1),
    ("el", 2), ("mmx", 6), ("mmc", 6), ("fp", 5), ("outa", 1), ("outb", 1),
    ("rs2", 3), ("fw", 4), ("fw2", 5), ("rs1", 6), ("outa", 5), ("o2a", 0),
    ("fw", 2), ("o2a", 1), ("fp", 2), ("outb", 5), ("el", 3), ("fp", 4),
    ("fw2", 4), ("o2b", 0), ("outa", 4), ("o2a", 5), ("rs2", 6), ("outb", 4),
    ("fw2", 2), ("fw", 3), ("o2b", 4), ("outa", 2), ("fp", 3), ("el", 6),
    ("outb", 2), ("fw2", 3), ("o2a", 4), ("o3b", 0), ("outa", 3), ("outb", 3),
    ("fw", 6), ("o3b", 4), ("grad2", 0), ("o2b", 3), ("o3a", 4), ("o2b", 1),
    ("fp", 6), ("o2a", 2), ("fw2", 6), ("o3a", 3), ("o3a", 0), ("o2a", 3),
    ("o2b", 2), ("outa", 6), ("outb", 6), ("grad1", 0), ("o3a", 2), ("grad2", 1),
    ("o3b", 1), ("o3a", 1), ("o3b", 2), ("o3b", 3), ("fin_send", 0), ("grad0", 0),
    ("o2a", 6), ("o2b", 5), ("grad0", 1), ("grad1", 1), ("o3a", 5), ("o3b", 5),
    ("sent", 0), ("end", 0),
)


def nt(a, b):
    return lax.dot_general(a, b, (((1,), (1,)), ((), ())), preferred_element_type=F32)


def nn(a, b):
    return jnp.dot(a, b, preferred_element_type=F32)


def tn(a, b):
    return lax.dot_general(a, b, (((0,), (0,)), ((), ())), preferred_element_type=F32)


def fold(v):
    v = v.reshape(v.shape[0] // 8, 8, W)
    return jnp.concatenate([v[:, :, :HALF], v[:, :, HALF:]], axis=1)


def unfold(v):
    v = jnp.concatenate([v[:, :8], v[:, 8:]], axis=2)
    return v.reshape(v.shape[0] * 8, W)


def kernel(plan, x_hbm, c_hbm, wg_hbm, wu_hbm, wd_hbm,
           out_ref, gt_ref, gg_hbm, gu_hbm, gd_hbm,
           x_in, c_in, acc, grad, wg, wu, wd, xc, xg, csnd, crcv, part, zsnd, zrcv, hid,
           pf, psnd, p1rcv, sf, s1snd, s1own, p2rcv, fin, frcv,
           ssem, rsem, lsem, gsem):
    depth, row, xx = lax.axis_index("depth"), lax.axis_index("row"), lax.axis_index("col")
    zl, y, zh, a = depth // 4, depth % 4, row // 2, row % 2
    nxt, prv, opp = (zh + 1 + 2 * a) % 4, (zh + 3 + 2 * a) % 4, (zh + 2) % 4

    def dev(zl_=zl, y_=y, zh_=zh, a_=a, x_=xx):
        return (zl_ * 4 + y_, zh_ * 2 + a_, x_)

    others = ([dev(zl_=1 - zl), dev(a_=1 - a), dev(zh_=nxt), dev(zh_=prv), dev(zh_=opp)]
              + [dev(x_=(xx + j) % 4) for j in (1, 2, 3)]
              + [dev(y_=(y + j) % 4) for j in (1, 2, 3)])
    mine = pl.ds(pl.multiple_of(a * HALF, 128), HALF)
    theirs = pl.ds(pl.multiple_of((1 - a) * HALF, 128), HALF)
    beside = y + 1 - 2 * (y % 2)
    here, there = 2 * (y // 2), 2 - 2 * (y // 2)
    size = [UNIT if part == WHOLE else UNIT // 2 for _, part in CHUNKS]

    def rows(i):
        return slice(sum(size[:i]), sum(size[:i + 1]))

    def quarter(i):
        return slice(sum(size[:i]) // 4, sum(size[:i + 1]) // 4)

    def piece(i, q):
        n = size[i] // 4
        return pl.ds(pl.multiple_of(sum(size[:i]) + n * q, 16), n)

    def chips(i):
        return {WHOLE: pl.ds(0, 4), NEAR: pl.ds(here, 2), FAR: pl.ds(there, 2)}[CHUNKS[i][1]]

    def slots(i):
        return {WHOLE: slice(0, 4), NEAR: slice(0, 2), FAR: slice(2, 4)}[CHUNKS[i][1]]

    def peers(i):
        return {WHOLE: [((y + j) % 4, j - 1) for j in (1, 2, 3)], NEAR: [(beside, 0)],
                FAR: [(there, 1 + y % 2), (there + 1, 1 + y % 2)]}[CHUNKS[i][1]]

    def heard(i):
        return {WHOLE: slice(0, 3), NEAR: slice(0, 1), FAR: slice(1, 3)}[CHUNKS[i][1]]

    def chunks(e):
        return [i for i, (u, _) in enumerate(CHUNKS) if u == e]

    across = [((xx + j) % 4, j - 1) for j in (1, 2, 3)]
    order = {}

    def at(i, k):
        return order.setdefault((i, k), len(order))

    def push(ssem_at, rsem_at, src, dst, to):
        pltpu.make_async_remote_copy(
            src_ref=src, dst_ref=dst, send_sem=ssem.at[ssem_at], recv_sem=rsem.at[rsem_at],
            device_id=to, device_id_type=pl.DeviceIdType.MESH).start()

    def send(i, k, src, dst, to):
        push(k, at(i, k), src, dst, to)

    def wait(sem, ref):
        pltpu.make_async_copy(ref, ref, sem).wait()

    def got(i, k, ref):
        wait(rsem.at[at(i, k)], ref)

    last = RECVS - 4

    barrier = pltpu.get_barrier_semaphore()
    for o in others:
        pl.semaphore_signal(barrier, inc=1, device_id=o, device_id_type=pl.DeviceIdType.MESH)
    loads = [pltpu.make_async_copy(s, d, lsem.at[j])
             for j, (s, d) in enumerate(((x_hbm, x_in), (c_hbm, c_in), (wg_hbm, wg),
                                         (wu_hbm, wu), (wd_hbm, wd)))]
    for ld in loads:
        ld.start()
    for k, ref in enumerate((x_in, c_in)):
        loads[k].wait()
        v = fold(ref[...].astype(F32)).astype(BF16)
        for u in range(3):
            xc[k, OWN[u], y, xx] = v[u]
    pl.semaphore_wait(barrier, len(others))

    def zl_send(u):
        push(KINDS, last + ZL + u,
             xc.at[:, OWN[u], y, xx], xc.at[:, OTHER[u], y, xx], dev(zl_=1 - zl))

    def ag1(e):
        if e in OTHER:
            wait(rsem.at[last + ZL + OTHER.index(e)], xc.at[:, e, y, xx])
        blk = xc.at[0, e, y, xx]
        for to, _ in across:
            send(chunks(e)[0], X1, blk, blk, dev(x_=to))
        blk = xc.at[1, e, y, xx]
        for i in chunks(e):
            for to, _ in peers(i):
                send(i, C1, blk, blk, dev(y_=to))

    def ag2x(i):
        e = CHUNKS[i][0]
        if i == chunks(e)[0]:
            got(i, X1, xc.at[0, e, y, :3])
        blk = xc.at[0, e, y]
        for to, _ in peers(i):
            send(i, X2, blk, blk, dev(y_=to))

    def ag2c(i):
        e = CHUNKS[i][0]
        got(i, C1, xc.at[1, e, heard(i), xx])
        blk = xc.at[1, e, chips(i), xx]
        for to, _ in across:
            send(i, C2, blk, blk, dev(x_=to))

    def ready(_):
        for ld in loads[2:]:
            ld.wait()

    def gathered(i, k):
        v = xc[k, CHUNKS[i][0], chips(i)].reshape(size[i] // 8, 16, HALF)
        v = unfold(v.astype(F32)).astype(BF16)
        xg[k, rows(i)] = v
        return v

    def mmx(i):
        rs = rows(i)
        got(i, X2, xc.at[0, CHUNKS[i][0], heard(i)])
        xs = gathered(i, 0)
        for j, w in ((0, wg), (1, wu)):
            csnd[j, rs] = nn(xs, w[:, theirs])
            send(i, CORE, csnd.at[j, rs], crcv.at[j, rs], dev(a_=1 - a))
        part[0, rs] = nn(xs, wg[:, mine])
        part[1, rs] = nn(xs, wu[:, mine])

    def mmc(i):
        rs = rows(i)
        got(i, C2, xc.at[1, CHUNKS[i][0], slots(i), :3])
        cs = gathered(i, 1)
        csnd[2, rs] = nt(cs, wd[theirs, :])
        send(i, CORE, csnd.at[2, rs], crcv.at[2, rs], dev(a_=1 - a))
        part[2, rs] = nt(cs, wd[mine, :])

    def rs1(i):
        rs, qs = rows(i), quarter(i)
        got(i, CORE, crcv.at[:, rs])
        part[:, rs] = part[:, rs] + crcv[:, rs]
        zsnd[0, :, qs] = part[:, piece(i, opp)].astype(BF16)
        send(i, ZA, zsnd.at[0, :, qs], zrcv.at[0, :, qs], dev(zh_=nxt))
        zsnd[1, :, qs] = part[:, piece(i, prv)].astype(BF16)
        send(i, ZB, zsnd.at[1, :, qs], zrcv.at[1, :, qs], dev(zh_=prv))

    def rs2(i):
        qs = quarter(i)
        got(i, ZA, zrcv.at[0, :, qs])
        zsnd[2, :, qs] = (part[:, piece(i, nxt)] + zrcv[0, :, qs].astype(F32)).astype(BF16)
        send(i, ZC, zsnd.at[2, :, qs], zrcv.at[2, :, qs], dev(zh_=nxt))

    def el(i):
        qs, ps = quarter(i), piece(i, zh)
        got(i, ZB, zrcv.at[1, :, qs])
        got(i, ZC, zrcv.at[2, :, qs])
        tot = part[:, ps] + zrcv[1, :, qs].astype(F32) + zrcv[2, :, qs].astype(F32)
        gate, up, slope = tot[0], tot[1], tot[2]
        sig = 1.0 / (1.0 + jnp.exp(-gate))
        act = gate * sig
        hid[0, ps, mine] = (act * up).astype(BF16)
        hid[1, ps, mine] = (slope * up * sig * (1.0 + gate * (1.0 - sig))).astype(BF16)
        hid[2, ps, mine] = (slope * act).astype(BF16)
        blk = hid.at[:, ps, mine]
        send(i, GN, blk, blk, dev(zh_=nxt))
        send(i, GP, blk, blk, dev(zh_=prv))
        if i in DIRECT:
            send(i, GF, blk, blk, dev(zh_=opp))
        send(i, GC, blk, blk, dev(a_=1 - a))

    def fw(i):
        blk = hid.at[:, piece(i, prv), mine]
        got(i, GN, blk)
        if i not in DIRECT:
            send(i, GF, blk, blk, dev(zh_=nxt))
        send(i, GC, blk, blk, dev(a_=1 - a))

    def fp(i):
        blk = hid.at[:, piece(i, nxt), mine]
        got(i, GP, blk)
        send(i, GC, blk, blk, dev(a_=1 - a))

    def fw2(i):
        blk = hid.at[:, piece(i, opp), mine]
        got(i, GF, blk)
        send(i, GC, blk, blk, dev(a_=1 - a))

    def outa(i):
        rs, e, ys = rows(i), CHUNKS[i][0], chips(i)
        got(i, GC, hid.at[:, rs, theirs])
        p = fold(nn(hid[0, rs], wd[...])).reshape(-1, 4, 16, HALF)
        pf[0, e, ys] = p
        psnd[0, e, ys] = p.astype(BF16)
        for to, j in across:
            send(i, O1, psnd.at[0, e, ys, to], p1rcv.at[0, j, e, slots(i)], dev(x_=to))

    def outb(i):
        rs, e, ys = rows(i), CHUNKS[i][0], chips(i)
        p = fold(nt(hid[1, rs], wg[...]) + nt(hid[2, rs], wu[...])).reshape(-1, 4, 16, HALF)
        pf[1, e, ys] = p
        psnd[1, e, ys] = p.astype(BF16)
        for to, j in peers(i):
            send(i, G1, psnd.at[1, e, to], p1rcv.at[1, j, e], dev(y_=to))

    def o2a(i):
        e, part = CHUNKS[i]
        got(i, O1, p1rcv.at[0, :, e, slots(i)])
        t = pf[0, e, chips(i), xx]
        for j in range(3):
            t = t + p1rcv[0, j, e, slots(i)].astype(F32)
        sf[slots(i)] = t
        s1snd[0, e, slots(i)] = t.astype(BF16)
        first = {WHOLE: 0, NEAR: here, FAR: there - 2}[part]
        for to, j in peers(i):
            send(i, O2, s1snd.at[0, e, to - first], p2rcv.at[0, j, e], dev(y_=to))
        if part != FAR:
            s1own[0, e] = sf[y - first]

    def o2b(e):
        for i in chunks(e):
            got(i, G1, p1rcv.at[1, heard(i), e])
        t = pf[1, e, y]
        for j in range(3):
            t = t + p1rcv[1, j, e].astype(F32)
        sf[...] = t
        s1snd[1, e] = t.astype(BF16)
        for to, j in across:
            send(chunks(e)[0], G2, s1snd.at[1, e, to], p2rcv.at[1, j, e], dev(x_=to))
        s1own[1, e] = sf[xx]

    def third(e, k):
        t = s1own[k, e]
        for j in range(3):
            t = t + p2rcv[k, j, e].astype(F32)
        fin[k, e] = t

    def o3a(e):
        for i in chunks(e):
            got(i, O2, p2rcv.at[0, heard(i), e])
        third(e, 0)

    def o3b(e):
        got(chunks(e)[0], G2, p2rcv.at[1, :, e])
        third(e, 1)

    def fin_send(_):
        push(KINDS + 1, last + FIN, fin.at[:, OTHER[0]:OTHER[-1] + 1], frcv, dev(zl_=1 - zl))

    def sent(_):
        block, half = xc.at[0, :, 0, :3], hid.at[:, :, :HALF]
        for k, ref in ((X1, block), (C1, block), (X2, xc.at[0, :, :3]), (C2, xc.at[1, :, :3]),
                       (CORE, csnd), (ZA, zsnd.at[0]), (ZB, zsnd.at[1]), (ZC, zsnd.at[2]),
                       (GN, zsnd.at[0]), (GP, zsnd.at[1]), (GF, zsnd.at[2]), (GC, half),
                       (O1, p1rcv.at[0]), (G1, p1rcv.at[1]), (O2, p2rcv.at[0]),
                       (G2, p2rcv.at[1]), (KINDS, xc.at[:, :3, 0, 0]), (KINDS + 1, frcv)):
            wait(ssem.at[k], ref)

    scale = W ** -0.5
    stores = []

    def grads(i, which):
        rs = slice(512 * i, 512 + 256 * i)
        lhs, rhs, res = ((xg.at[0, rs], hid[1, rs], gg_hbm), (xg.at[0, rs], hid[2, rs], gu_hbm),
                         (hid.at[0, rs], xg[1, rs], gd_hbm))[which]

        def tile(n, _):
            ds = pl.ds(pl.multiple_of(n * 256, 256), 256)
            t = tn(lhs[:, ds], rhs)
            if i == 0:
                acc[which, ds, :] = t
            else:
                grad[which, ds, :] = ((t + acc[which, ds, :]) * scale).astype(BF16)
            return _

        lax.fori_loop(0, 3, tile, 0)
        if i == 1:
            st = pltpu.make_async_copy(grad.at[which], res, gsem.at[which])
            st.start()
            stores.append(st)

    def grad0(i):
        grads(i, 0)

    def grad1(i):
        grads(i, 1)

    def grad2(i):
        grads(i, 2)

    def end(_):
        wait(rsem.at[last + FIN], frcv)
        for k, ref in enumerate((out_ref, gt_ref)):
            v = jnp.stack([fin[k, e] for e in OWN]) + frcv[k]
            ref[...] = unfold(v).astype(BF16)

    steps = {f.__name__: f for f in (
        zl_send, ag1, ag2x, ag2c, ready, mmx, mmc, rs1, rs2, el, fw, fp, fw2, outa, outb,
        o2a, o2b, o3a, o3b, fin_send, sent, grad0, grad1, grad2, end)}
    for name, i in plan:
        steps[name](i)
    for st in stores:
        st.wait()


def move(*refs):
    srcs, dsts, bufs, isem, osem = refs[:5], refs[5:10], refs[10:15], refs[15], refs[16]
    parts = []
    for j in (2, 3, 4):
        for q in range(2):
            ds = pl.ds(q * HALF, HALF)
            parts.append((srcs[j].at[ds], bufs[j].at[ds], dsts[j].at[ds]))
    for j in (0, 1):
        parts.append((srcs[j], bufs[j], dsts[j]))
    loads = [pltpu.make_async_copy(s, b, isem.at[n]) for n, (s, b, _) in enumerate(parts)]
    stores = [pltpu.make_async_copy(b, d, osem.at[n]) for n, (_, b, d) in enumerate(parts)]
    for ld in loads:
        ld.start()
    for ld, st in zip(loads, stores):
        ld.wait()
        st.start()
    for st in stores:
        st.wait()


def local(tokens, cotangent, gate_weight, up_weight, down_weight):
    vmem = pl.BlockSpec(memory_space=pltpu.VMEM)
    hbm = pl.BlockSpec(memory_space=pl.ANY)
    small = jax.ShapeDtypeStruct((LOCAL, W), BF16)
    big = jax.ShapeDtypeStruct((W, W), BF16)
    results = pl.pallas_call(
        functools.partial(kernel, PLAN),
        name="swiglu",
        out_shape=(small, small, big, big, big),
        in_specs=[hbm] * 5,
        out_specs=(vmem, vmem, hbm, hbm, hbm),
        scratch_shapes=[
            pltpu.VMEM((LOCAL, W), BF16),
            pltpu.VMEM((LOCAL, W), BF16),
            pltpu.VMEM((3, W, W), F32),
            pltpu.VMEM((3, W, W), BF16),
            pltpu.VMEM((W, W), BF16),
            pltpu.VMEM((W, W), BF16),
            pltpu.VMEM((W, W), BF16),
            pltpu.VMEM((2, 6, 4, 4, 16, HALF), BF16),
            pltpu.VMEM((2, W, W), BF16),
            pltpu.VMEM((3, W, HALF), F32),
            pltpu.VMEM((3, W, HALF), F32),
            pltpu.VMEM((3, W, HALF), F32),
            pltpu.VMEM((3, 3, W // 4, HALF), BF16),
            pltpu.VMEM((3, 3, W // 4, HALF), BF16),
            pltpu.VMEM((3, W, W), BF16),
            pltpu.VMEM((2, 6, 4, 4, 16, HALF), F32),
            pltpu.VMEM((2, 6, 4, 4, 16, HALF), BF16),
            pltpu.VMEM((2, 3, 6, 4, 16, HALF), BF16),
            pltpu.VMEM((4, 16, HALF), F32),
            pltpu.VMEM((2, 6, 4, 16, HALF), BF16),
            pltpu.VMEM((2, 6, 16, HALF), F32),
            pltpu.VMEM((2, 3, 6, 16, HALF), BF16),
            pltpu.VMEM((2, 6, 16, HALF), F32),
            pltpu.VMEM((2, 3, 16, HALF), F32),
            pltpu.SemaphoreType.DMA((SENDS,)),
            pltpu.SemaphoreType.DMA((RECVS,)),
            pltpu.SemaphoreType.DMA((5,)),
            pltpu.SemaphoreType.DMA((3,)),
        ],
        compiler_params=pltpu.CompilerParams(
            collective_id=0, has_side_effects=True, vmem_limit_bytes=56 << 20),
        cost_estimate=pl.CostEstimate(
            flops=18 * W ** 3, bytes_accessed=12 * W * W, transcendentals=W * W // 8),
    )(tokens, cotangent, gate_weight, up_weight, down_weight)
    return pl.pallas_call(
        move,
        name="move",
        out_shape=(small, small, big, big, big),
        in_specs=[hbm] * 5,
        out_specs=(hbm,) * 5,
        scratch_shapes=[pltpu.VMEM((LOCAL, W), BF16)] * 2 + [pltpu.VMEM((W, W), BF16)] * 3
        + [pltpu.SemaphoreType.DMA((8,))] * 2,
        compiler_params=pltpu.CompilerParams(vmem_limit_bytes=60 << 20),
    )(*results)


def solution(mesh):
    by_token = P(("depth", "col"), "row")
    by_model = P("row", ("depth", "col"))
    return jax.shard_map(
        local,
        mesh=mesh,
        in_specs=(by_token, by_token, by_model, by_model, by_token),
        out_specs=(by_token, by_token, by_model, by_model, by_token),
        check_vma=False,
    )
```

```python
import functools

import jax
import jax.numpy as jnp
from jax import lax
from jax.experimental import pallas as pl
from jax.experimental.pallas import tpu as pltpu
from jax.sharding import PartitionSpec as P

F32 = jnp.float32
BF16 = jnp.bfloat16
W = 768
HALF = W // 2
LOCAL = 24
UNIT = 128

OWN = (0, 4, 5)
OTHER = (1, 2, 3)
WHOLE, NEAR, FAR = range(3)
CHUNKS = ((0, NEAR), (0, FAR), (1, WHOLE), (2, WHOLE), (3, WHOLE), (4, WHOLE), (5, WHOLE))

X1, C1, X2, C2, CORE, ZA, ZB, ZC, GN, GP, GF, GC, O1, G1, O2, G2 = range(16)
KINDS = 16
ZL, FIN = 0, 3
SENDS = KINDS + 2
RECVS = 14 * len(CHUNKS) + 2 * 6 + 4

PLAN = (
    ("ag1", 0), ("zl_send", 2), ("ag1", 4), ("ag2x", 0), ("ag2c", 0), ("zl_send", 1),
    ("ready", 0), ("ag2x", 1), ("zl_send", 0), ("ag2c", 1), ("ag1", 3), ("ag2x", 5),
    ("ag2c", 5), ("mmx", 0), ("mmc", 0), ("ag2x", 4), ("rs1", 0), ("mmc", 1),
    ("mmx", 1), ("ag2c", 4), ("mmx", 5), ("rs1", 1), ("mmc", 5), ("ag1", 1),
    ("ag1", 5), ("rs2", 0), ("rs1", 5), ("mmx", 4), ("ag1", 2), ("mmc", 4),
    ("ag2x", 2), ("rs2", 1), ("ag2c", 2), ("el", 0), ("rs1", 4), ("el", 1),
    ("rs2", 5), ("mmx", 2), ("ag2x", 3), ("mmc", 2), ("ag2c", 3), ("fw", 0),
    ("rs1", 2), ("fw", 1), ("mmx", 3), ("rs2", 4), ("mmc", 3), ("el", 5),
    ("rs2", 2), ("ag2x", 6), ("ag2c", 6), ("rs1", 3), ("fp", 0), ("fw2", 0),
    ("outa", 0), ("el", 4), ("outb", 0), ("fw", 5), ("fw2", 1), ("fp", 1),
    ("el", 2), ("mmx", 6), ("mmc", 6), ("fp", 5), ("outa", 1), ("outb", 1),
    ("rs2", 3), ("fw", 4), ("fw2", 5), ("rs1", 6), ("outa", 5), ("o2a", 0),
    ("fw", 2), ("o2a", 1), ("fp", 2), ("outb", 5), ("el", 3), ("fp", 4),
    ("fw2", 4), ("o2b", 0), ("outa", 4), ("o2a", 5), ("rs2", 6), ("outb", 4),
    ("fw2", 2), ("fw", 3), ("o2b", 4), ("outa", 2), ("fp", 3), ("el", 6),
    ("outb", 2), ("fw2", 3), ("o2a", 4), ("o3b", 0), ("outa", 3), ("outb", 3),
    ("fw", 6), ("o3b", 4), ("grad2", 0), ("o2b", 3), ("o3a", 4), ("o2b", 1),
    ("fp", 6), ("o2a", 2), ("fw2", 6), ("o3a", 3), ("o3a", 0), ("o2a", 3),
    ("o2b", 2), ("outa", 6), ("outb", 6), ("grad1", 0), ("o3a", 2), ("grad2", 1),
    ("o3b", 1), ("o3a", 1), ("o3b", 2), ("o3b", 3), ("fin_send", 0), ("grad0", 0),
    ("o2a", 6), ("o2b", 5), ("grad0", 1), ("grad1", 1), ("o3a", 5), ("o3b", 5),
    ("sent", 0), ("end", 0),
)


def nt(a, b):
    return lax.dot_general(a, b, (((1,), (1,)), ((), ())), preferred_element_type=F32)


def nn(a, b):
    return jnp.dot(a, b, preferred_element_type=F32)


def tn(a, b):
    return lax.dot_general(a, b, (((0,), (0,)), ((), ())), preferred_element_type=F32)


def fold(v):
    v = v.reshape(v.shape[0] // 8, 8, W)
    return jnp.concatenate([v[:, :, :HALF], v[:, :, HALF:]], axis=1)


def unfold(v):
    v = jnp.concatenate([v[:, :8], v[:, 8:]], axis=2)
    return v.reshape(v.shape[0] * 8, W)


def kernel(plan, x_hbm, c_hbm, wg_hbm, wu_hbm, wd_hbm,
           out_ref, gt_ref, gg_hbm, gu_hbm, gd_hbm,
           x_in, c_in, acc, grad, wg, wu, wd, xc, xg, csnd, crcv, part, zsnd, zrcv, hid,
           pf, psnd, p1rcv, sf, s1snd, s1own, p2rcv, fin, frcv,
           ssem, rsem, lsem, gsem):
    depth, row, xx = lax.axis_index("depth"), lax.axis_index("row"), lax.axis_index("col")
    zl, y, zh, a = depth // 4, depth % 4, row // 2, row % 2
    nxt, prv, opp = (zh + 1 + 2 * a) % 4, (zh + 3 + 2 * a) % 4, (zh + 2) % 4

    def dev(zl_=zl, y_=y, zh_=zh, a_=a, x_=xx):
        return (zl_ * 4 + y_, zh_ * 2 + a_, x_)

    others = ([dev(zl_=1 - zl), dev(a_=1 - a), dev(zh_=nxt), dev(zh_=prv)]
              + [dev(x_=(xx + j) % 4) for j in (1, 2, 3)]
              + [dev(y_=(y + j) % 4) for j in (1, 2, 3)])
    mine = pl.ds(pl.multiple_of(a * HALF, 128), HALF)
    theirs = pl.ds(pl.multiple_of((1 - a) * HALF, 128), HALF)
    beside = y + 1 - 2 * (y % 2)
    here, there = 2 * (y // 2), 2 - 2 * (y // 2)
    size = [UNIT if part == WHOLE else UNIT // 2 for _, part in CHUNKS]

    def rows(i):
        return slice(sum(size[:i]), sum(size[:i + 1]))

    def quarter(i):
        return slice(sum(size[:i]) // 4, sum(size[:i + 1]) // 4)

    def piece(i, q):
        n = size[i] // 4
        return pl.ds(pl.multiple_of(sum(size[:i]) + n * q, 16), n)

    def chips(i):
        return {WHOLE: pl.ds(0, 4), NEAR: pl.ds(here, 2), FAR: pl.ds(there, 2)}[CHUNKS[i][1]]

    def slots(i):
        return {WHOLE: slice(0, 4), NEAR: slice(0, 2), FAR: slice(2, 4)}[CHUNKS[i][1]]

    def peers(i):
        return {WHOLE: [((y + j) % 4, j - 1) for j in (1, 2, 3)], NEAR: [(beside, 0)],
                FAR: [(there, 1 + y % 2), (there + 1, 1 + y % 2)]}[CHUNKS[i][1]]

    def heard(i):
        return {WHOLE: slice(0, 3), NEAR: slice(0, 1), FAR: slice(1, 3)}[CHUNKS[i][1]]

    def chunks(e):
        return [i for i, (u, _) in enumerate(CHUNKS) if u == e]

    across = [((xx + j) % 4, j - 1) for j in (1, 2, 3)]
    order = {}

    def at(i, k):
        return order.setdefault((i, k), len(order))

    def push(ssem_at, rsem_at, src, dst, to):
        pltpu.make_async_remote_copy(
            src_ref=src, dst_ref=dst, send_sem=ssem.at[ssem_at], recv_sem=rsem.at[rsem_at],
            device_id=to, device_id_type=pl.DeviceIdType.MESH).start()

    def send(i, k, src, dst, to):
        push(k, at(i, k), src, dst, to)

    def wait(sem, ref):
        pltpu.make_async_copy(ref, ref, sem).wait()

    def got(i, k, ref):
        wait(rsem.at[at(i, k)], ref)

    last = RECVS - 4

    barrier = pltpu.get_barrier_semaphore()
    for o in others:
        pl.semaphore_signal(barrier, inc=1, device_id=o, device_id_type=pl.DeviceIdType.MESH)
    loads = [pltpu.make_async_copy(s, d, lsem.at[j])
             for j, (s, d) in enumerate(((x_hbm, x_in), (c_hbm, c_in), (wg_hbm, wg),
                                         (wu_hbm, wu), (wd_hbm, wd)))]
    for ld in loads:
        ld.start()
    for k, ref in enumerate((x_in, c_in)):
        loads[k].wait()
        v = fold(ref[...].astype(F32)).astype(BF16)
        for u in range(3):
            xc[k, OWN[u], y, xx] = v[u]
    pl.semaphore_wait(barrier, len(others))

    def zl_send(u):
        push(KINDS, last + ZL + u,
             xc.at[:, OWN[u], y, xx], xc.at[:, OTHER[u], y, xx], dev(zl_=1 - zl))

    def ag1(e):
        if e in OTHER:
            wait(rsem.at[last + ZL + OTHER.index(e)], xc.at[:, e, y, xx])
        blk = xc.at[0, e, y, xx]
        for to, _ in across:
            send(chunks(e)[0], X1, blk, blk, dev(x_=to))
        blk = xc.at[1, e, y, xx]
        for i in chunks(e):
            for to, _ in peers(i):
                send(i, C1, blk, blk, dev(y_=to))

    def ag2x(i):
        e = CHUNKS[i][0]
        if i == chunks(e)[0]:
            got(i, X1, xc.at[0, e, y, :3])
        blk = xc.at[0, e, y]
        for to, _ in peers(i):
            send(i, X2, blk, blk, dev(y_=to))

    def ag2c(i):
        e = CHUNKS[i][0]
        got(i, C1, xc.at[1, e, heard(i), xx])
        blk = xc.at[1, e, chips(i), xx]
        for to, _ in across:
            send(i, C2, blk, blk, dev(x_=to))

    def ready(_):
        for ld in loads[2:]:
            ld.wait()

    def gathered(i, k):
        v = xc[k, CHUNKS[i][0], chips(i)].reshape(size[i] // 8, 16, HALF)
        v = unfold(v.astype(F32)).astype(BF16)
        xg[k, rows(i)] = v
        return v

    def mmx(i):
        rs = rows(i)
        got(i, X2, xc.at[0, CHUNKS[i][0], heard(i)])
        xs = gathered(i, 0)
        for j, w in ((0, wg), (1, wu)):
            csnd[j, rs] = nn(xs, w[:, theirs])
            send(i, CORE, csnd.at[j, rs], crcv.at[j, rs], dev(a_=1 - a))
        part[0, rs] = nn(xs, wg[:, mine])
        part[1, rs] = nn(xs, wu[:, mine])

    def mmc(i):
        rs = rows(i)
        got(i, C2, xc.at[1, CHUNKS[i][0], slots(i), :3])
        cs = gathered(i, 1)
        csnd[2, rs] = nt(cs, wd[theirs, :])
        send(i, CORE, csnd.at[2, rs], crcv.at[2, rs], dev(a_=1 - a))
        part[2, rs] = nt(cs, wd[mine, :])

    def rs1(i):
        rs, qs = rows(i), quarter(i)
        got(i, CORE, crcv.at[:, rs])
        part[:, rs] = part[:, rs] + crcv[:, rs]
        zsnd[0, :, qs] = part[:, piece(i, opp)].astype(BF16)
        send(i, ZA, zsnd.at[0, :, qs], zrcv.at[0, :, qs], dev(zh_=nxt))
        zsnd[1, :, qs] = part[:, piece(i, prv)].astype(BF16)
        send(i, ZB, zsnd.at[1, :, qs], zrcv.at[1, :, qs], dev(zh_=prv))

    def rs2(i):
        qs = quarter(i)
        got(i, ZA, zrcv.at[0, :, qs])
        zsnd[2, :, qs] = (part[:, piece(i, nxt)] + zrcv[0, :, qs].astype(F32)).astype(BF16)
        send(i, ZC, zsnd.at[2, :, qs], zrcv.at[2, :, qs], dev(zh_=nxt))

    def el(i):
        qs, ps = quarter(i), piece(i, zh)
        got(i, ZB, zrcv.at[1, :, qs])
        got(i, ZC, zrcv.at[2, :, qs])
        tot = part[:, ps] + zrcv[1, :, qs].astype(F32) + zrcv[2, :, qs].astype(F32)
        gate, up, slope = tot[0], tot[1], tot[2]
        sig = 1.0 / (1.0 + jnp.exp(-gate))
        act = gate * sig
        hid[0, ps, mine] = (act * up).astype(BF16)
        hid[1, ps, mine] = (slope * up * sig * (1.0 + gate * (1.0 - sig))).astype(BF16)
        hid[2, ps, mine] = (slope * act).astype(BF16)
        blk = hid.at[:, ps, mine]
        send(i, GN, blk, blk, dev(zh_=nxt))
        send(i, GP, blk, blk, dev(zh_=prv))
        send(i, GC, blk, blk, dev(a_=1 - a))

    def fw(i):
        blk = hid.at[:, piece(i, prv), mine]
        got(i, GN, blk)
        send(i, GF, blk, blk, dev(zh_=nxt))
        send(i, GC, blk, blk, dev(a_=1 - a))

    def fp(i):
        blk = hid.at[:, piece(i, nxt), mine]
        got(i, GP, blk)
        send(i, GC, blk, blk, dev(a_=1 - a))

    def fw2(i):
        blk = hid.at[:, piece(i, opp), mine]
        got(i, GF, blk)
        send(i, GC, blk, blk, dev(a_=1 - a))

    def outa(i):
        rs, e, ys = rows(i), CHUNKS[i][0], chips(i)
        got(i, GC, hid.at[:, rs, theirs])
        p = fold(nn(hid[0, rs], wd[...])).reshape(-1, 4, 16, HALF)
        pf[0, e, ys] = p
        psnd[0, e, ys] = p.astype(BF16)
        for to, j in across:
            send(i, O1, psnd.at[0, e, ys, to], p1rcv.at[0, j, e, slots(i)], dev(x_=to))

    def outb(i):
        rs, e, ys = rows(i), CHUNKS[i][0], chips(i)
        p = fold(nt(hid[1, rs], wg[...]) + nt(hid[2, rs], wu[...])).reshape(-1, 4, 16, HALF)
        pf[1, e, ys] = p
        psnd[1, e, ys] = p.astype(BF16)
        for to, j in peers(i):
            send(i, G1, psnd.at[1, e, to], p1rcv.at[1, j, e], dev(y_=to))

    def o2a(i):
        e, part = CHUNKS[i]
        got(i, O1, p1rcv.at[0, :, e, slots(i)])
        t = pf[0, e, chips(i), xx]
        for j in range(3):
            t = t + p1rcv[0, j, e, slots(i)].astype(F32)
        sf[slots(i)] = t
        s1snd[0, e, slots(i)] = t.astype(BF16)
        first = {WHOLE: 0, NEAR: here, FAR: there - 2}[part]
        for to, j in peers(i):
            send(i, O2, s1snd.at[0, e, to - first], p2rcv.at[0, j, e], dev(y_=to))
        if part != FAR:
            s1own[0, e] = sf[y - first]

    def o2b(e):
        for i in chunks(e):
            got(i, G1, p1rcv.at[1, heard(i), e])
        t = pf[1, e, y]
        for j in range(3):
            t = t + p1rcv[1, j, e].astype(F32)
        sf[...] = t
        s1snd[1, e] = t.astype(BF16)
        for to, j in across:
            send(chunks(e)[0], G2, s1snd.at[1, e, to], p2rcv.at[1, j, e], dev(x_=to))
        s1own[1, e] = sf[xx]

    def third(e, k):
        t = s1own[k, e]
        for j in range(3):
            t = t + p2rcv[k, j, e].astype(F32)
        fin[k, e] = t

    def o3a(e):
        for i in chunks(e):
            got(i, O2, p2rcv.at[0, heard(i), e])
        third(e, 0)

    def o3b(e):
        got(chunks(e)[0], G2, p2rcv.at[1, :, e])
        third(e, 1)

    def fin_send(_):
        push(KINDS + 1, last + FIN, fin.at[:, OTHER[0]:OTHER[-1] + 1], frcv, dev(zl_=1 - zl))

    def sent(_):
        block, half = xc.at[0, :, 0, :3], hid.at[:, :, :HALF]
        for k, ref in ((X1, block), (C1, block), (X2, xc.at[0, :, :3]), (C2, xc.at[1, :, :3]),
                       (CORE, csnd), (ZA, zsnd.at[0]), (ZB, zsnd.at[1]), (ZC, zsnd.at[2]),
                       (GN, zsnd.at[0]), (GP, zsnd.at[1]), (GF, zsnd.at[2]), (GC, half),
                       (O1, p1rcv.at[0]), (G1, p1rcv.at[1]), (O2, p2rcv.at[0]),
                       (G2, p2rcv.at[1]), (KINDS, xc.at[:, :3, 0, 0]), (KINDS + 1, frcv)):
            wait(ssem.at[k], ref)

    scale = W ** -0.5
    stores = []

    def grads(i, which):
        rs = slice(512 * i, 512 + 256 * i)
        lhs, rhs, res = ((xg.at[0, rs], hid[1, rs], gg_hbm), (xg.at[0, rs], hid[2, rs], gu_hbm),
                         (hid.at[0, rs], xg[1, rs], gd_hbm))[which]

        def tile(n, _):
            ds = pl.ds(pl.multiple_of(n * 256, 256), 256)
            t = tn(lhs[:, ds], rhs)
            if i == 0:
                acc[which, ds, :] = t
            else:
                grad[which, ds, :] = ((t + acc[which, ds, :]) * scale).astype(BF16)
            return _

        lax.fori_loop(0, 3, tile, 0, unroll=True)
        if i == 1:
            st = pltpu.make_async_copy(grad.at[which], res, gsem.at[which])
            st.start()
            stores.append(st)

    def grad0(i):
        grads(i, 0)

    def grad1(i):
        grads(i, 1)

    def grad2(i):
        grads(i, 2)

    def end(_):
        wait(rsem.at[last + FIN], frcv)
        for k, ref in enumerate((out_ref, gt_ref)):
            v = jnp.stack([fin[k, e] for e in OWN]) + frcv[k]
            ref[...] = unfold(v).astype(BF16)

    steps = {f.__name__: f for f in (
        zl_send, ag1, ag2x, ag2c, ready, mmx, mmc, rs1, rs2, el, fw, fp, fw2, outa, outb,
        o2a, o2b, o3a, o3b, fin_send, sent, grad0, grad1, grad2, end)}
    for name, i in plan:
        steps[name](i)
    for st in stores:
        st.wait()


def move(*refs):
    srcs, dsts, bufs, isem, osem = refs[:5], refs[5:10], refs[10:15], refs[15], refs[16]
    parts = []
    for j in (2, 3, 4):
        for q in range(2):
            ds = pl.ds(q * HALF, HALF)
            parts.append((srcs[j].at[ds], bufs[j].at[ds], dsts[j].at[ds]))
    for j in (0, 1):
        parts.append((srcs[j], bufs[j], dsts[j]))
    loads = [pltpu.make_async_copy(s, b, isem.at[n]) for n, (s, b, _) in enumerate(parts)]
    stores = [pltpu.make_async_copy(b, d, osem.at[n]) for n, (_, b, d) in enumerate(parts)]
    for ld in loads:
        ld.start()
    for ld, st in zip(loads, stores):
        ld.wait()
        st.start()
    for st in stores:
        st.wait()


def local(tokens, cotangent, gate_weight, up_weight, down_weight):
    vmem = pl.BlockSpec(memory_space=pltpu.VMEM)
    hbm = pl.BlockSpec(memory_space=pl.ANY)
    small = jax.ShapeDtypeStruct((LOCAL, W), BF16)
    big = jax.ShapeDtypeStruct((W, W), BF16)
    results = pl.pallas_call(
        functools.partial(kernel, PLAN),
        name="swiglu",
        out_shape=(small, small, big, big, big),
        in_specs=[hbm] * 5,
        out_specs=(vmem, vmem, hbm, hbm, hbm),
        scratch_shapes=[
            pltpu.VMEM((LOCAL, W), BF16),
            pltpu.VMEM((LOCAL, W), BF16),
            pltpu.VMEM((3, W, W), F32),
            pltpu.VMEM((3, W, W), BF16),
            pltpu.VMEM((W, W), BF16),
            pltpu.VMEM((W, W), BF16),
            pltpu.VMEM((W, W), BF16),
            pltpu.VMEM((2, 6, 4, 4, 16, HALF), BF16),
            pltpu.VMEM((2, W, W), BF16),
            pltpu.VMEM((3, W, HALF), F32),
            pltpu.VMEM((3, W, HALF), F32),
            pltpu.VMEM((3, W, HALF), F32),
            pltpu.VMEM((3, 3, W // 4, HALF), BF16),
            pltpu.VMEM((3, 3, W // 4, HALF), BF16),
            pltpu.VMEM((3, W, W), BF16),
            pltpu.VMEM((2, 6, 4, 4, 16, HALF), F32),
            pltpu.VMEM((2, 6, 4, 4, 16, HALF), BF16),
            pltpu.VMEM((2, 3, 6, 4, 16, HALF), BF16),
            pltpu.VMEM((4, 16, HALF), F32),
            pltpu.VMEM((2, 6, 4, 16, HALF), BF16),
            pltpu.VMEM((2, 6, 16, HALF), F32),
            pltpu.VMEM((2, 3, 6, 16, HALF), BF16),
            pltpu.VMEM((2, 6, 16, HALF), F32),
            pltpu.VMEM((2, 3, 16, HALF), F32),
            pltpu.SemaphoreType.DMA((SENDS,)),
            pltpu.SemaphoreType.DMA((RECVS,)),
            pltpu.SemaphoreType.DMA((5,)),
            pltpu.SemaphoreType.DMA((3,)),
        ],
        compiler_params=pltpu.CompilerParams(
            collective_id=0, has_side_effects=True, vmem_limit_bytes=56 << 20),
        cost_estimate=pl.CostEstimate(
            flops=18 * W ** 3, bytes_accessed=12 * W * W, transcendentals=W * W // 8),
    )(tokens, cotangent, gate_weight, up_weight, down_weight)
    return pl.pallas_call(
        move,
        name="move",
        out_shape=(small, small, big, big, big),
        in_specs=[hbm] * 5,
        out_specs=(hbm,) * 5,
        scratch_shapes=[pltpu.VMEM((LOCAL, W), BF16)] * 2 + [pltpu.VMEM((W, W), BF16)] * 3
        + [pltpu.SemaphoreType.DMA((8,))] * 2,
        compiler_params=pltpu.CompilerParams(vmem_limit_bytes=60 << 20),
    )(*results)


def solution(mesh):
    by_token = P(("depth", "col"), "row")
    by_model = P("row", ("depth", "col"))
    return jax.shard_map(
        local,
        mesh=mesh,
        in_specs=(by_token, by_token, by_model, by_model, by_token),
        out_specs=(by_token, by_token, by_model, by_model, by_token),
        check_vma=False,
    )
```

```python
import functools

import jax
import jax.numpy as jnp
from jax import lax
from jax.experimental import pallas as pl
from jax.experimental.pallas import tpu as pltpu
from jax.sharding import PartitionSpec as P

F32 = jnp.float32
BF16 = jnp.bfloat16
W = 768
HALF = W // 2
LOCAL = 24
UNIT = 128

OWN = (0, 4, 5)
OTHER = (1, 2, 3)
WHOLE, NEAR, FAR = range(3)
CHUNKS = ((0, NEAR), (0, FAR), (1, WHOLE), (2, WHOLE), (3, WHOLE), (4, WHOLE), (5, WHOLE))

X1, C1, X2, C2, CORE, ZA, ZB, ZC, GN, GP, GF, GC, O1, G1, O2, G2 = range(16)
KINDS = 16
ZL, FIN = 0, 3
SENDS = KINDS + 2
RECVS = 13 * len(CHUNKS) + 2 * 6 + 4

PLAN = (
    ("ag1", 0), ("zl_send", 2), ("ag1", 4), ("ag2x", 0), ("ag2c", 0), ("zl_send", 1),
    ("ready", 0), ("ag2x", 1), ("zl_send", 0), ("ag2c", 1), ("ag1", 3), ("ag2x", 5),
    ("ag2c", 5), ("mmx", 0), ("mmc", 0), ("ag2x", 4), ("rs1", 0), ("mmc", 1),
    ("mmx", 1), ("ag2c", 4), ("mmx", 5), ("rs1", 1), ("mmc", 5), ("ag1", 1),
    ("ag1", 5), ("rs2", 0), ("rs1", 5), ("mmx", 4), ("ag1", 2), ("mmc", 4),
    ("ag2x", 2), ("rs2", 1), ("ag2c", 2), ("el", 0), ("rs1", 4), ("el", 1),
    ("rs2", 5), ("mmx", 2), ("ag2x", 3), ("mmc", 2), ("ag2c", 3), ("fw", 0),
    ("rs1", 2), ("fw", 1), ("mmx", 3), ("rs2", 4), ("mmc", 3), ("el", 5),
    ("rs2", 2), ("ag2x", 6), ("ag2c", 6), ("rs1", 3), ("fp", 0), ("fw2", 0),
    ("outa", 0), ("el", 4), ("outb", 0), ("fw", 5), ("fw2", 1), ("fp", 1),
    ("el", 2), ("mmx", 6), ("mmc", 6), ("fp", 5), ("outa", 1), ("outb", 1),
    ("rs2", 3), ("fw", 4), ("fw2", 5), ("rs1", 6), ("outa", 5), ("o2a", 0),
    ("fw", 2), ("o2a", 1), ("fp", 2), ("outb", 5), ("el", 3), ("fp", 4),
    ("fw2", 4), ("o2b", 0), ("outa", 4), ("o2a", 5), ("rs2", 6), ("outb", 4),
    ("fw2", 2), ("fw", 3), ("o2b", 4), ("outa", 2), ("fp", 3), ("el", 6),
    ("outb", 2), ("fw2", 3), ("o2a", 4), ("o3b", 0), ("outa", 3), ("outb", 3),
    ("fw", 6), ("o3b", 4), ("grad2", 0), ("o2b", 3), ("o3a", 4), ("o2b", 1),
    ("fp", 6), ("o2a", 2), ("fw2", 6), ("o3a", 3), ("o3a", 0), ("o2a", 3),
    ("o2b", 2), ("outa", 6), ("outb", 6), ("grad1", 0), ("o3a", 2), ("grad2", 1),
    ("o3b", 1), ("o3a", 1), ("o3b", 2), ("o3b", 3), ("fin_send", 0), ("grad0", 0),
    ("o2a", 6), ("o2b", 5), ("grad0", 1), ("grad1", 1), ("o3a", 5), ("o3b", 5),
    ("sent", 0), ("end", 0),
)


def nt(a, b):
    return lax.dot_general(a, b, (((1,), (1,)), ((), ())), preferred_element_type=F32)


def nn(a, b):
    return jnp.dot(a, b, preferred_element_type=F32)


def tn(a, b):
    return lax.dot_general(a, b, (((0,), (0,)), ((), ())), preferred_element_type=F32)


def fold(v):
    v = v.reshape(v.shape[0] // 8, 8, W)
    return jnp.concatenate([v[:, :, :HALF], v[:, :, HALF:]], axis=1)


def unfold(v):
    v = jnp.concatenate([v[:, :8], v[:, 8:]], axis=2)
    return v.reshape(v.shape[0] * 8, W)


def kernel(plan, x_hbm, c_hbm, wg_hbm, wu_hbm, wd_hbm,
           out_ref, gt_ref, gg_hbm, gu_hbm, gd_hbm,
           x_in, c_in, acc, grad, wg, wu, wd, xc, xg, csnd, crcv, part, zsnd, zrcv, hid,
           pf, psnd, p1rcv, sf, s1snd, s1own, p2rcv, fin, frcv,
           ssem, rsem, lsem, gsem):
    depth, row, xx = lax.axis_index("depth"), lax.axis_index("row"), lax.axis_index("col")
    zl, y, zh, a = depth // 4, depth % 4, row // 2, row % 2
    nxt, prv, opp = (zh + 1 + 2 * a) % 4, (zh + 3 + 2 * a) % 4, (zh + 2) % 4

    def dev(zl_=zl, y_=y, zh_=zh, a_=a, x_=xx):
        return (zl_ * 4 + y_, zh_ * 2 + a_, x_)

    others = ([dev(zl_=1 - zl), dev(a_=1 - a), dev(zh_=nxt), dev(zh_=prv)]
              + [dev(x_=(xx + j) % 4) for j in (1, 2, 3)]
              + [dev(y_=(y + j) % 4) for j in (1, 2, 3)])
    mine = pl.ds(pl.multiple_of(a * HALF, 128), HALF)
    theirs = pl.ds(pl.multiple_of((1 - a) * HALF, 128), HALF)
    beside = y + 1 - 2 * (y % 2)
    here, there = 2 * (y // 2), 2 - 2 * (y // 2)
    size = [UNIT if part == WHOLE else UNIT // 2 for _, part in CHUNKS]

    def rows(i):
        return slice(sum(size[:i]), sum(size[:i + 1]))

    def quarter(i):
        return slice(sum(size[:i]) // 4, sum(size[:i + 1]) // 4)

    def piece(i, q):
        n = size[i] // 4
        return pl.ds(pl.multiple_of(sum(size[:i]) + n * q, 16), n)

    def chips(i):
        return {WHOLE: pl.ds(0, 4), NEAR: pl.ds(here, 2), FAR: pl.ds(there, 2)}[CHUNKS[i][1]]

    def slots(i):
        return {WHOLE: slice(0, 4), NEAR: slice(0, 2), FAR: slice(2, 4)}[CHUNKS[i][1]]

    def peers(i):
        return {WHOLE: [((y + j) % 4, j - 1) for j in (1, 2, 3)], NEAR: [(beside, 0)],
                FAR: [(there, 1 + y % 2), (there + 1, 1 + y % 2)]}[CHUNKS[i][1]]

    def heard(i):
        return {WHOLE: slice(0, 3), NEAR: slice(0, 1), FAR: slice(1, 3)}[CHUNKS[i][1]]

    def chunks(e):
        return [i for i, (u, _) in enumerate(CHUNKS) if u == e]

    across = [((xx + j) % 4, j - 1) for j in (1, 2, 3)]
    order = {}

    def at(i, k):
        return order.setdefault((i, k), len(order))

    def push(ssem_at, rsem_at, src, dst, to):
        pltpu.make_async_remote_copy(
            src_ref=src, dst_ref=dst, send_sem=ssem.at[ssem_at], recv_sem=rsem.at[rsem_at],
            device_id=to, device_id_type=pl.DeviceIdType.MESH).start()

    def send(i, k, src, dst, to):
        push(k, at(i, k), src, dst, to)

    def wait(sem, ref):
        pltpu.make_async_copy(ref, ref, sem).wait()

    def got(i, k, ref):
        wait(rsem.at[at(i, k)], ref)

    last = RECVS - 4

    barrier = pltpu.get_barrier_semaphore()
    for o in others:
        pl.semaphore_signal(barrier, inc=1, device_id=o, device_id_type=pl.DeviceIdType.MESH)
    loads = [pltpu.make_async_copy(s, d, lsem.at[j])
             for j, (s, d) in enumerate(((x_hbm, x_in), (c_hbm, c_in), (wg_hbm, wg),
                                         (wu_hbm, wu), (wd_hbm, wd)))]
    for ld in loads:
        ld.start()
    for k, ref in enumerate((x_in, c_in)):
        loads[k].wait()
        v = fold(ref[...].astype(F32)).astype(BF16)
        for u in range(3):
            xc[k, OWN[u], y, xx] = v[u]
    pl.semaphore_wait(barrier, len(others))

    def zl_send(u):
        push(KINDS, last + ZL + u,
             xc.at[:, OWN[u], y, xx], xc.at[:, OTHER[u], y, xx], dev(zl_=1 - zl))

    def ag1(e):
        if e in OTHER:
            wait(rsem.at[last + ZL + OTHER.index(e)], xc.at[:, e, y, xx])
        blk = xc.at[0, e, y, xx]
        for to, _ in across:
            send(chunks(e)[0], X1, blk, blk, dev(x_=to))
        blk = xc.at[1, e, y, xx]
        for i in chunks(e):
            for to, _ in peers(i):
                send(i, C1, blk, blk, dev(y_=to))

    def ag2x(i):
        e = CHUNKS[i][0]
        if i == chunks(e)[0]:
            got(i, X1, xc.at[0, e, y, :3])
        blk = xc.at[0, e, y]
        for to, _ in peers(i):
            send(i, X2, blk, blk, dev(y_=to))

    def ag2c(i):
        e = CHUNKS[i][0]
        got(i, C1, xc.at[1, e, heard(i), xx])
        blk = xc.at[1, e, chips(i), xx]
        for to, _ in across:
            send(i, C2, blk, blk, dev(x_=to))

    def ready(_):
        for ld in loads[2:]:
            ld.wait()

    def gathered(i, k):
        v = xc[k, CHUNKS[i][0], chips(i)].reshape(size[i] // 8, 16, HALF)
        v = unfold(v.astype(F32)).astype(BF16)
        xg[k, rows(i)] = v
        return v

    def mmx(i):
        rs = rows(i)
        got(i, X2, xc.at[0, CHUNKS[i][0], heard(i)])
        xs = gathered(i, 0)
        for j, w in ((0, wg), (1, wu)):
            csnd[j, rs] = nn(xs, w[:, theirs])
            send(i, CORE, csnd.at[j, rs], crcv.at[j, rs], dev(a_=1 - a))
        part[0, rs] = nn(xs, wg[:, mine])
        part[1, rs] = nn(xs, wu[:, mine])

    def mmc(i):
        rs = rows(i)
        got(i, C2, xc.at[1, CHUNKS[i][0], slots(i), :3])
        cs = gathered(i, 1)
        csnd[2, rs] = nt(cs, wd[theirs, :])
        send(i, CORE, csnd.at[2, rs], crcv.at[2, rs], dev(a_=1 - a))
        part[2, rs] = nt(cs, wd[mine, :])

    def rs1(i):
        rs, qs = rows(i), quarter(i)
        got(i, CORE, crcv.at[:, rs])
        part[:, rs] = part[:, rs] + crcv[:, rs]
        zsnd[0, :, qs] = part[:, piece(i, opp)].astype(BF16)
        send(i, ZA, zsnd.at[0, :, qs], zrcv.at[0, :, qs], dev(zh_=nxt))
        zsnd[1, :, qs] = part[:, piece(i, prv)].astype(BF16)
        send(i, ZB, zsnd.at[1, :, qs], zrcv.at[1, :, qs], dev(zh_=prv))

    def rs2(i):
        qs = quarter(i)
        got(i, ZA, zrcv.at[0, :, qs])
        zsnd[2, :, qs] = (part[:, piece(i, nxt)] + zrcv[0, :, qs].astype(F32)).astype(BF16)
        push(ZC, at(i, ZB), zsnd.at[2, :, qs], zrcv.at[2, :, qs], dev(zh_=nxt))

    def el(i):
        qs, ps = quarter(i), piece(i, zh)
        got(i, ZB, zrcv.at[1:, :, qs])
        tot = part[:, ps] + zrcv[1, :, qs].astype(F32) + zrcv[2, :, qs].astype(F32)
        gate, up, slope = tot[0], tot[1], tot[2]
        sig = 1.0 / (1.0 + jnp.exp(-gate))
        act = gate * sig
        hid[0, ps, mine] = (act * up).astype(BF16)
        hid[1, ps, mine] = (slope * up * sig * (1.0 + gate * (1.0 - sig))).astype(BF16)
        hid[2, ps, mine] = (slope * act).astype(BF16)
        blk = hid.at[:, ps, mine]
        send(i, GN, blk, blk, dev(zh_=nxt))
        send(i, GP, blk, blk, dev(zh_=prv))
        send(i, GC, blk, blk, dev(a_=1 - a))

    def fw(i):
        blk = hid.at[:, piece(i, prv), mine]
        got(i, GN, blk)
        send(i, GF, blk, blk, dev(zh_=nxt))
        send(i, GC, blk, blk, dev(a_=1 - a))

    def fp(i):
        blk = hid.at[:, piece(i, nxt), mine]
        got(i, GP, blk)
        send(i, GC, blk, blk, dev(a_=1 - a))

    def fw2(i):
        blk = hid.at[:, piece(i, opp), mine]
        got(i, GF, blk)
        send(i, GC, blk, blk, dev(a_=1 - a))

    def outa(i):
        rs, e, ys = rows(i), CHUNKS[i][0], chips(i)
        got(i, GC, hid.at[:, rs, theirs])
        p = fold(nn(hid[0, rs], wd[...])).reshape(-1, 4, 16, HALF)
        pf[0, e, ys] = p
        psnd[0, e, ys] = p.astype(BF16)
        for to, j in across:
            send(i, O1, psnd.at[0, e, ys, to], p1rcv.at[0, j, e, slots(i)], dev(x_=to))

    def outb(i):
        rs, e, ys = rows(i), CHUNKS[i][0], chips(i)
        p = fold(nt(hid[1, rs], wg[...]) + nt(hid[2, rs], wu[...])).reshape(-1, 4, 16, HALF)
        pf[1, e, ys] = p
        psnd[1, e, ys] = p.astype(BF16)
        for to, j in peers(i):
            send(i, G1, psnd.at[1, e, to], p1rcv.at[1, j, e], dev(y_=to))

    def o2a(i):
        e, part = CHUNKS[i]
        got(i, O1, p1rcv.at[0, :, e, slots(i)])
        t = pf[0, e, chips(i), xx]
        for j in range(3):
            t = t + p1rcv[0, j, e, slots(i)].astype(F32)
        sf[slots(i)] = t
        s1snd[0, e, slots(i)] = t.astype(BF16)
        first = {WHOLE: 0, NEAR: here, FAR: there - 2}[part]
        for to, j in peers(i):
            send(i, O2, s1snd.at[0, e, to - first], p2rcv.at[0, j, e], dev(y_=to))
        if part != FAR:
            s1own[0, e] = sf[y - first]

    def o2b(e):
        for i in chunks(e):
            got(i, G1, p1rcv.at[1, heard(i), e])
        t = pf[1, e, y]
        for j in range(3):
            t = t + p1rcv[1, j, e].astype(F32)
        sf[...] = t
        s1snd[1, e] = t.astype(BF16)
        for to, j in across:
            send(chunks(e)[0], G2, s1snd.at[1, e, to], p2rcv.at[1, j, e], dev(x_=to))
        s1own[1, e] = sf[xx]

    def third(e, k):
        t = s1own[k, e]
        for j in range(3):
            t = t + p2rcv[k, j, e].astype(F32)
        fin[k, e] = t

    def o3a(e):
        for i in chunks(e):
            got(i, O2, p2rcv.at[0, heard(i), e])
        third(e, 0)

    def o3b(e):
        got(chunks(e)[0], G2, p2rcv.at[1, :, e])
        third(e, 1)

    def fin_send(_):
        push(KINDS + 1, last + FIN, fin.at[:, OTHER[0]:OTHER[-1] + 1], frcv, dev(zl_=1 - zl))

    def sent(_):
        block, half = xc.at[0, :, 0, :3], hid.at[:, :, :HALF]
        for k, ref in ((X1, block), (C1, block), (X2, xc.at[0, :, :3]), (C2, xc.at[1, :, :3]),
                       (CORE, csnd), (ZA, zsnd.at[0]), (ZB, zsnd.at[1]), (ZC, zsnd.at[2]),
                       (GN, zsnd.at[0]), (GP, zsnd.at[1]), (GF, zsnd.at[2]), (GC, half),
                       (O1, p1rcv.at[0]), (G1, p1rcv.at[1]), (O2, p2rcv.at[0]),
                       (G2, p2rcv.at[1]), (KINDS, xc.at[:, :3, 0, 0]), (KINDS + 1, frcv)):
            wait(ssem.at[k], ref)

    scale = W ** -0.5
    stores = []

    def grads(i, which):
        rs = slice(512 * i, 512 + 256 * i)
        lhs, rhs, res = ((xg.at[0, rs], hid[1, rs], gg_hbm), (xg.at[0, rs], hid[2, rs], gu_hbm),
                         (hid.at[0, rs], xg[1, rs], gd_hbm))[which]

        def tile(n, _):
            ds = pl.ds(pl.multiple_of(n * 256, 256), 256)
            t = tn(lhs[:, ds], rhs)
            if i == 0:
                acc[which, ds, :] = t
            else:
                grad[which, ds, :] = ((t + acc[which, ds, :]) * scale).astype(BF16)
            return _

        lax.fori_loop(0, 3, tile, 0, unroll=True)
        if i == 1:
            st = pltpu.make_async_copy(grad.at[which], res, gsem.at[which])
            st.start()
            stores.append(st)

    def grad0(i):
        grads(i, 0)

    def grad1(i):
        grads(i, 1)

    def grad2(i):
        grads(i, 2)

    def end(_):
        wait(rsem.at[last + FIN], frcv)
        for k, ref in enumerate((out_ref, gt_ref)):
            v = jnp.stack([fin[k, e] for e in OWN]) + frcv[k]
            ref[...] = unfold(v).astype(BF16)

    steps = {f.__name__: f for f in (
        zl_send, ag1, ag2x, ag2c, ready, mmx, mmc, rs1, rs2, el, fw, fp, fw2, outa, outb,
        o2a, o2b, o3a, o3b, fin_send, sent, grad0, grad1, grad2, end)}
    for name, i in plan:
        steps[name](i)
    for st in stores:
        st.wait()


def move(*refs):
    srcs, dsts, bufs, isem, osem = refs[:5], refs[5:10], refs[10:15], refs[15], refs[16]
    parts = []
    for j in (2, 3, 4):
        for q in range(2):
            ds = pl.ds(q * HALF, HALF)
            parts.append((srcs[j].at[ds], bufs[j].at[ds], dsts[j].at[ds]))
    for j in (0, 1):
        parts.append((srcs[j], bufs[j], dsts[j]))
    loads = [pltpu.make_async_copy(s, b, isem.at[n]) for n, (s, b, _) in enumerate(parts)]
    stores = [pltpu.make_async_copy(b, d, osem.at[n]) for n, (_, b, d) in enumerate(parts)]
    for ld in loads:
        ld.start()
    for ld, st in zip(loads, stores):
        ld.wait()
        st.start()
    for st in stores:
        st.wait()


def local(tokens, cotangent, gate_weight, up_weight, down_weight):
    vmem = pl.BlockSpec(memory_space=pltpu.VMEM)
    hbm = pl.BlockSpec(memory_space=pl.ANY)
    small = jax.ShapeDtypeStruct((LOCAL, W), BF16)
    big = jax.ShapeDtypeStruct((W, W), BF16)
    results = pl.pallas_call(
        functools.partial(kernel, PLAN),
        name="swiglu",
        out_shape=(small, small, big, big, big),
        in_specs=[hbm] * 5,
        out_specs=(vmem, vmem, hbm, hbm, hbm),
        scratch_shapes=[
            pltpu.VMEM((LOCAL, W), BF16),
            pltpu.VMEM((LOCAL, W), BF16),
            pltpu.VMEM((3, W, W), F32),
            pltpu.VMEM((3, W, W), BF16),
            pltpu.VMEM((W, W), BF16),
            pltpu.VMEM((W, W), BF16),
            pltpu.VMEM((W, W), BF16),
            pltpu.VMEM((2, 6, 4, 4, 16, HALF), BF16),
            pltpu.VMEM((2, W, W), BF16),
            pltpu.VMEM((3, W, HALF), F32),
            pltpu.VMEM((3, W, HALF), F32),
            pltpu.VMEM((3, W, HALF), F32),
            pltpu.VMEM((3, 3, W // 4, HALF), BF16),
            pltpu.VMEM((3, 3, W // 4, HALF), BF16),
            pltpu.VMEM((3, W, W), BF16),
            pltpu.VMEM((2, 6, 4, 4, 16, HALF), F32),
            pltpu.VMEM((2, 6, 4, 4, 16, HALF), BF16),
            pltpu.VMEM((2, 3, 6, 4, 16, HALF), BF16),
            pltpu.VMEM((4, 16, HALF), F32),
            pltpu.VMEM((2, 6, 4, 16, HALF), BF16),
            pltpu.VMEM((2, 6, 16, HALF), F32),
            pltpu.VMEM((2, 3, 6, 16, HALF), BF16),
            pltpu.VMEM((2, 6, 16, HALF), F32),
            pltpu.VMEM((2, 3, 16, HALF), F32),
            pltpu.SemaphoreType.DMA((SENDS,)),
            pltpu.SemaphoreType.DMA((RECVS,)),
            pltpu.SemaphoreType.DMA((5,)),
            pltpu.SemaphoreType.DMA((3,)),
        ],
        compiler_params=pltpu.CompilerParams(
            collective_id=0, has_side_effects=True, vmem_limit_bytes=56 << 20),
        cost_estimate=pl.CostEstimate(
            flops=18 * W ** 3, bytes_accessed=12 * W * W, transcendentals=W * W // 8),
    )(tokens, cotangent, gate_weight, up_weight, down_weight)
    return pl.pallas_call(
        move,
        name="move",
        out_shape=(small, small, big, big, big),
        in_specs=[hbm] * 5,
        out_specs=(hbm,) * 5,
        scratch_shapes=[pltpu.VMEM((LOCAL, W), BF16)] * 2 + [pltpu.VMEM((W, W), BF16)] * 3
        + [pltpu.SemaphoreType.DMA((8,))] * 2,
        compiler_params=pltpu.CompilerParams(vmem_limit_bytes=60 << 20),
    )(*results)


def solution(mesh):
    by_token = P(("depth", "col"), "row")
    by_model = P("row", ("depth", "col"))
    return jax.shard_map(
        local,
        mesh=mesh,
        in_specs=(by_token, by_token, by_model, by_model, by_token),
        out_specs=(by_token, by_token, by_model, by_model, by_token),
        check_vma=False,
    )
```
